512 devices in a mesh: rows: 32 (over z, core), cols: 16 (over x, y).
Axes of the slice: x: 4, y: 4, z: 16, core: 2. Of those that a mesh axis runs over, the one named last changes fastest.
Arguments:
- tile_values: bfloat16 [16384, 256, 256], P(('rows', 'cols')), may hold values from 0 to 30, as said below
- tile_rows: int32 [16384], P(('rows', 'cols')), may hold values from 0 to 15, as said below
- tile_cols: int32 [16384], P(('rows', 'cols')), may hold values from 0 to 31, as said below
- live_count: int32 [512], P(('rows', 'cols')), may hold values from 16 to 32, as said below
- initial: bfloat16 [131072, 128], P(('rows', 'cols')), may hold values from -6 to 6
Outputs:
- basis: float32 [131072, 128], P(('rows', 'cols'))
The draws below stay inside these ranges and needn't reach their ends.
Inputs may be any that keep to these rules, and one draw needn't show every extreme that they name: `tile_values`: every row and every column of each tile holds a positive entry. `tile_rows`: on every device the first 16 slots name each of its block rows once; further slots favour low block rows. `tile_cols`: slot 0 of the device at rows index r names block column r. `live_count`: some device has all 32 slots live.
All inputs are finite; a program needn't handle non-finite values.
Results may differ from the reference program's by a relative error of at most 0.02.
Values may be sent and summed in bfloat16 or wider, within the bound.
No kernel may reach another device: no remote copies, remote signals or barrier semaphores. Data moves between devices by JAX's collectives and lax.ppermute only.
A program may use at most 64 MiB of HBM per device.

```python
import math
import jax
import jax.numpy as jnp
from jax import lax

TILE = 256
RANK = 128
SLOTS = 32
ITERS = 2
RBLK = 16
GCOL = 32
BLOCKS = 512
NODES = 131072


def spread_factor(key, shape, lowest):
    return jnp.exp(jax.random.uniform(key, shape, jnp.float32, math.log(lowest), 0.0))


def draw_tile_values(key, part):
    key = jax.random.fold_in(key, 14)
    row_groups = BLOCKS // RBLK

    def one_device(index):
        device_key = jax.random.fold_in(key, index)
        perm_key, mask_key, weight_key, row_key, col_key = jax.random.split(device_key, 5)
        slot_keys = jax.random.split(perm_key, SLOTS)
        orders = jax.vmap(lambda one: jax.random.permutation(one, TILE))(slot_keys).astype(jnp.int32)
        columns = jnp.arange(TILE, dtype=jnp.int32)
        placed = orders[:, :, None] == columns[None, None, :]
        scattered = jax.random.randint(mask_key, (SLOTS, TILE, TILE), 0, TILE) < 4
        present = jnp.logical_or(placed, scattered)
        group = (index // RBLK).astype(jnp.float32)
        level = jnp.exp(math.log(30.0) * group / jnp.float32(max(row_groups - 1, 1)))
        weight = spread_factor(weight_key, (SLOTS, TILE, TILE), 0.1)
        row_factor = spread_factor(row_key, (SLOTS, TILE, 1), 0.3)
        col_factor = spread_factor(col_key, (SLOTS, 1, TILE), 0.3)
        values = jnp.where(present, level * weight * row_factor * col_factor, jnp.float32(0.0))
        return values.astype(jnp.bfloat16)
    tiles = lax.map(one_device, jnp.arange(BLOCKS, dtype=jnp.int32))
    return tiles.reshape(BLOCKS * SLOTS, TILE, TILE)


def draw_tile_rows(key, part):
    key = jax.random.fold_in(key, 11)
    first_key, second_key, third_key = jax.random.split(key, 3)
    device_keys = jax.random.split(first_key, BLOCKS)
    leading = jax.vmap(lambda one: jax.random.permutation(one, RBLK))(device_keys).astype(jnp.int32)
    extra_one = jax.random.randint(second_key, (BLOCKS, SLOTS - RBLK), 0, RBLK)
    extra_two = jax.random.randint(third_key, (BLOCKS, SLOTS - RBLK), 0, RBLK)
    extra = jnp.minimum(extra_one, extra_two).astype(jnp.int32)
    return jnp.concatenate([leading, extra], axis=1).reshape(BLOCKS * SLOTS).astype(jnp.int32)


def draw_tile_cols(key, part):
    key = jax.random.fold_in(key, 12)
    diagonal = (jnp.arange(BLOCKS, dtype=jnp.int32) // RBLK)[:, None]
    others = jax.random.randint(key, (BLOCKS, SLOTS - 1), 0, GCOL).astype(jnp.int32)
    return jnp.concatenate([diagonal, others], axis=1).reshape(BLOCKS * SLOTS).astype(jnp.int32)


def draw_live_count(key, part):
    key = jax.random.fold_in(key, 13)
    first_key, second_key, third_key = jax.random.split(key, 3)
    count_one = jax.random.randint(first_key, (BLOCKS,), RBLK, SLOTS + 1)
    count_two = jax.random.randint(second_key, (BLOCKS,), RBLK, SLOTS + 1)
    counts = jnp.minimum(count_one, count_two)
    fullest = jax.random.randint(third_key, (), 0, BLOCKS)
    counts = jnp.where(jnp.arange(BLOCKS) == fullest, SLOTS, counts)
    return counts.astype(jnp.int32)


def block_scale(rng, shape, pieces, least, high):
    level = 1.0
    for axis_at, blocks in pieces:
        heights = jax.random.uniform(jax.random.fold_in(jax.random.fold_in(rng, 6), axis_at), (blocks,), jnp.float32, least / len(pieces), high / len(pieces))
        level = level * jnp.repeat(jnp.exp(heights), shape[axis_at] // blocks).reshape((-1,) + (1,) * (len(shape) - 1 - axis_at))
    return level


def noise(stream_key, dims, deviation, limit, cuts=(), held_as=jnp.bfloat16):
    entries = jax.random.normal(stream_key, dims, jnp.float32) * deviation
    if len(cuts) > 0:
        entries = block_scale(stream_key, dims, cuts, -0.22, 0.18) * entries
    return jnp.clip(entries, min=-limit, max=limit).astype(held_as)


def setup_inputs(seed: int = 0) -> dict:
    arg_keys = jax.random.split(jax.random.key(seed), 6)
    return {
        "tile_values": draw_tile_values(jax.random.fold_in(arg_keys[5], 71), 0),
        "tile_rows": draw_tile_rows(jax.random.fold_in(arg_keys[5], 71), 0),
        "tile_cols": draw_tile_cols(jax.random.fold_in(arg_keys[5], 71), 0),
        "live_count": draw_live_count(jax.random.fold_in(arg_keys[5], 71), 0),
        "initial": noise(arg_keys[4], (NODES, RANK), 1.0, 6.0, ((0, 512),)),
    }


def reference(tile_values, tile_rows, tile_cols, live_count, initial):
    tile_blocks = tile_values.reshape(BLOCKS, SLOTS, TILE, TILE)
    rows_local = tile_rows.reshape(BLOCKS, SLOTS).astype(jnp.int32)
    cols_local = tile_cols.reshape(BLOCKS, SLOTS).astype(jnp.int32)
    device = jnp.arange(BLOCKS, dtype=jnp.int32)
    live_mask = (jnp.arange(SLOTS, dtype=jnp.int32)[None, :] < live_count[:, None]).astype(jnp.float32)
    global_rows = (device // RBLK)[:, None] * RBLK + rows_local
    global_cols = cols_local * RBLK + (device % RBLK)[:, None]
    row_part = lax.optimization_barrier(jnp.sum(tile_blocks, axis=3, dtype=jnp.float32)) * live_mask[:, :, None]
    col_part = lax.optimization_barrier(jnp.sum(tile_blocks, axis=2, dtype=jnp.float32)) * live_mask[:, :, None]
    row_degree = jnp.zeros((BLOCKS, TILE), jnp.float32).at[global_rows.reshape(-1)].add(row_part.reshape(-1, TILE))
    col_degree = jnp.zeros((BLOCKS, TILE), jnp.float32).at[global_cols.reshape(-1)].add(col_part.reshape(-1, TILE))
    row_scale = lax.rsqrt(row_degree).reshape(NODES)
    col_scale = lax.rsqrt(col_degree)[:, :, None]
    current = initial
    basis = jnp.zeros((NODES, RANK), jnp.float32)
    for sweep in range(ITERS):
        scaled = (col_scale * current.reshape(BLOCKS, TILE, RANK).astype(jnp.float32)).astype(jnp.bfloat16)

        def device_step(total, item):
            tiles_here, cols_here, rows_here, mask_here, owner = item
            picked = scaled[cols_here]
            product = jnp.einsum('stu,suk->stk', tiles_here.astype(jnp.float32), picked.astype(jnp.float32), precision=lax.Precision.HIGHEST)
            product = product * mask_here[:, None, None]
            partial_value = jnp.zeros((RBLK, TILE, RANK), jnp.float32).at[rows_here].add(product)
            partial_value = lax.optimization_barrier(partial_value.astype(jnp.bfloat16)).astype(jnp.float32)
            first = (owner // RBLK * RBLK).astype(jnp.int32)
            present = lax.dynamic_slice_in_dim(total, first, RBLK, 0)
            return (lax.dynamic_update_slice_in_dim(total, present + partial_value, first, 0), None)
        total, unused = lax.scan(device_step, jnp.zeros((BLOCKS, TILE, RANK), jnp.float32), (tile_blocks, global_cols, rows_local, live_mask, device))
        fresh = row_scale[:, None] * total.reshape(NODES, RANK)
        gram = jnp.dot(fresh.T.astype(jnp.float32), fresh.astype(jnp.float32), precision=lax.Precision.HIGHEST, preferred_element_type=jnp.float32)
        lower = jnp.linalg.cholesky(gram)
        basis = lax.linalg.triangular_solve(lower, fresh, left_side=False, lower=True, transpose_a=True)
        current = basis.astype(jnp.bfloat16)
    return basis
```

```python
import functools

import jax
import jax.numpy as jnp
import numpy as np
from jax import lax
from jax.experimental import pallas as pl
from jax.experimental.pallas import tpu as pltpu
from jax.sharding import Mesh, PartitionSpec as P

ZS = 16
PEERS = 16
SIDE = 256
WIDTH = 128
FIRST = 16
EXTRA = 32
VMEM_BYTES = 48 * 1024 * 1024
F32 = jnp.float32
BF16 = jnp.bfloat16
HIGHEST = lax.Precision.HIGHEST

params = pltpu.CompilerParams(vmem_limit_bytes=VMEM_BYTES)
smem = pl.BlockSpec(memory_space=pltpu.SMEM)
vmem = pl.BlockSpec(memory_space=pltpu.VMEM)


def eye_mask():
    return lax.broadcasted_iota(jnp.int32, (WIDTH, WIDTH), 0) == lax.broadcasted_iota(
        jnp.int32, (WIDTH, WIDTH), 1
    )


def to_column(lanes):
    spread = jnp.broadcast_to(lanes, (WIDTH, WIDTH))
    return jnp.sum(jnp.where(eye_mask(), spread, 0.0), axis=1, keepdims=True)


def split3(value):
    high = value.astype(BF16)
    rest = value - high.astype(F32)
    middle = rest.astype(BF16)
    low = (rest - middle.astype(F32)).astype(BF16)
    return high, middle, low


def degree_kernel(cols_ref, live_ref, tiles_ref, out_ref, acc_ref):
    acc_ref[...] = jnp.zeros_like(acc_ref)

    def one(slot, carry):
        tile = tiles_ref[slot].astype(F32).reshape(SIDE // 8, 8, SIDE)
        acc_ref[cols_ref[slot]] += jnp.sum(tile, axis=0)
        return carry

    lax.fori_loop(0, live_ref[0], one, 0)
    out_ref[...] = jnp.zeros_like(out_ref)
    for block in range(2 * ZS):
        total = jnp.sum(acc_ref[block], axis=0, keepdims=True)
        at = 2 * (block % 2)
        out_ref[block // 2, at : at + 1, :] = total[:, :WIDTH]
        out_ref[block // 2, at + 1 : at + 2, :] = total[:, WIDTH:]


def scale_kernel(mine_ref, other_ref, initial_ref, out_ref, scale_ref):
    degree = mine_ref[...] + other_ref[...]
    scale = lax.rsqrt(degree)
    scale_ref[...] = scale
    for half in range(2):
        rows = slice(half * WIDTH, (half + 1) * WIDTH)
        column = to_column(scale[half : half + 1])
        scaled = (column * initial_ref[rows].astype(F32)).astype(BF16)
        for peer in range(ZS):
            out_ref[peer, rows] = scaled


def product_kernel(with_rows, core_ref, rows_ref, cols_ref, live_ref, tiles_ref, mine_ref, other_ref, out_ref, acc_ref):
    core = core_ref[0]

    def product(slot):
        col = cols_ref[slot]
        at = lax.div(col, 2)
        same = lax.rem(col, 2) == core
        block = jnp.where(same, mine_ref[at, :SIDE], other_ref[at, :SIDE])
        if with_rows:
            block = jnp.concatenate([block, jnp.ones((SIDE, WIDTH), BF16)], axis=1)
        return jnp.dot(tiles_ref[slot], block, preferred_element_type=F32)

    def first(slot, carry):
        acc_ref[rows_ref[slot]] = product(slot)
        return carry

    def later(slot, carry):
        acc_ref[rows_ref[slot]] += product(slot)
        return carry

    lax.fori_loop(0, FIRST, first, 0, unroll=4)
    lax.fori_loop(FIRST, live_ref[0], later, 0)
    if with_rows:
        eye = eye_mask()
        zero = jnp.zeros((EXTRA - 6, WIDTH), BF16)
        for block in range(PEERS):
            out_ref[block, :SIDE] = acc_ref[block, :, :WIDTH].astype(BF16)
            pieces = []
            for half in range(2):
                spread = acc_ref[block, half * WIDTH : (half + 1) * WIDTH, WIDTH:]
                pieces.append(jnp.sum(jnp.where(eye, spread, 0.0), axis=0, keepdims=True))
            parts = split3(jnp.concatenate(pieces, axis=0))
            out_ref[block, SIDE:] = jnp.concatenate(list(parts) + [zero], axis=0)
    else:
        gram = jnp.zeros((8, WIDTH), F32)
        for at in range(ZS):
            for ref in (mine_ref, other_ref):
                extra = ref[at, SIDE:].astype(F32)
                gram += extra[0:8] + extra[8:16] + extra[16:24]
        extra = jnp.concatenate(list(split3(gram)) + [jnp.zeros((8, WIDTH), BF16)], axis=0)
        for block in range(PEERS):
            out_ref[block, :SIDE] = acc_ref[block].astype(BF16)
            out_ref[block, SIDE:] = extra


def total_of(ref, rows):
    total = ref[0, rows].astype(F32)
    for peer in range(1, PEERS):
        total += ref[peer, rows].astype(F32)
    return total


def gram_of(fresh):
    return lax.dot_general(
        fresh, fresh, (((0,), (0,)), ((), ())), precision=HIGHEST, preferred_element_type=F32
    )


def middle_kernel(arrived_ref, col_scale_ref, out_ref, row_scale_ref):
    extra = total_of(arrived_ref, slice(SIDE, SIDE + EXTRA))
    degree = extra[0:2] + extra[2:4] + extra[4:6]
    row_scale = lax.rsqrt(degree)
    row_scale_ref[...] = row_scale
    halves = []
    for half in range(2):
        rows = slice(half * WIDTH, (half + 1) * WIDTH)
        fresh = to_column(row_scale[half : half + 1]) * total_of(arrived_ref, rows)
        halves.append(fresh)
        scaled = (to_column(col_scale_ref[half : half + 1]) * fresh).astype(BF16)
        for peer in range(ZS):
            out_ref[peer, rows] = scaled
    gram = gram_of(jnp.concatenate(halves, axis=0))
    zero = jnp.zeros((8, WIDTH), BF16)
    for peer in range(ZS):
        piece = gram[8 * peer : 8 * peer + 8]
        out_ref[peer, SIDE:] = jnp.concatenate(list(split3(piece)) + [zero], axis=0)


def last_kernel(arrived_ref, row_scale_ref, fresh_ref, gram_ref, first_gram_ref):
    halves = []
    for half in range(2):
        rows = slice(half * WIDTH, (half + 1) * WIDTH)
        fresh = to_column(row_scale_ref[half : half + 1]) * total_of(arrived_ref, rows)
        fresh_ref[rows] = fresh
        halves.append(fresh)
    gram_ref[...] = gram_of(jnp.concatenate(halves, axis=0))
    extra = total_of(arrived_ref, slice(SIDE, SIDE + EXTRA))
    first_gram_ref[...] = extra[0:8] + extra[8:16] + extra[16:24]


def lower_inverse(matrix):
    groups = WIDTH // 8
    parts = [matrix[8 * g : 8 * g + 8] for g in range(groups)]
    lane = lax.broadcasted_iota(jnp.int32, (8, WIDTH), 1)
    row = lax.broadcasted_iota(jnp.int32, (8, WIDTH), 0)
    roots = [jnp.zeros((8, WIDTH), F32) for _ in range(groups)]
    for k in range(WIDTH):
        g, r = divmod(k, 8)
        pivot_row = jnp.broadcast_to(parts[g][r : r + 1], (8, WIDTH))
        pivot = jnp.broadcast_to(parts[g][r : r + 1, k : k + 1], (8, WIDTH))
        roots[g] = jnp.where(row == r, pivot, roots[g])
        inverse = 1.0 / pivot
        at_k = lane == k
        source = jnp.where(at_k, 1.0, pivot_row) * inverse
        for h in range(g, groups):
            factor = jnp.broadcast_to(parts[h][:, k : k + 1], (8, WIDTH))
            kept = jnp.where(at_k, 0.0, parts[h])
            changed = kept - factor * source
            if h == g:
                parts[h] = jnp.where(row > r, changed, parts[h])
            else:
                parts[h] = changed
    out = []
    for g in range(groups):
        below = lane < row + 8 * g
        unit = jnp.where(below, parts[g], jnp.where(lane == row + 8 * g, 1.0, 0.0))
        out.append(unit * lax.rsqrt(roots[g]))
    return jnp.concatenate(out, axis=0)


def dot(a, b, dims):
    return lax.dot_general(a, b, (dims, ((), ())), precision=HIGHEST, preferred_element_type=F32)


def finish_kernel(first_gram_ref, gram_ref, fresh_ref, out_ref):
    first = lower_inverse(first_gram_ref[...])
    gram = dot(dot(first, gram_ref[...], ((1,), (0,))), first, ((1,), (1,)))
    second = lower_inverse(gram)
    fresh = dot(fresh_ref[...], first, ((1,), (1,)))
    out_ref[...] = dot(fresh, second, ((1,), (1,)))


def shape(dims, dtype):
    return jax.ShapeDtypeStruct(dims, dtype)


def shards(tile_values, tile_rows, tile_cols, live_count, initial):
    core = lax.axis_index("core")
    core_at = jnp.full((1,), core, jnp.int32)
    swap = [(0, 1), (1, 0)]

    with jax.named_scope("col_degree"):
        part = pl.pallas_call(
            degree_kernel,
            out_shape=shape((ZS, 8, WIDTH), F32),
            in_specs=[smem, smem, vmem],
            out_specs=vmem,
            scratch_shapes=[pltpu.VMEM((2 * ZS, 8, SIDE), F32)],
            compiler_params=params,
        )(tile_cols, live_count, tile_values)
        pieces = jnp.sum(lax.all_to_all(part, "z", 0, 0, tiled=True), axis=0)
        mine = lax.dynamic_slice_in_dim(pieces, 2 * core, 2, 0)
        other = lax.ppermute(lax.dynamic_slice_in_dim(pieces, 2 - 2 * core, 2, 0), "core", swap)
    with jax.named_scope("scale"):
        sent, col_scale = pl.pallas_call(
            scale_kernel,
            out_shape=(shape((ZS, SIDE, WIDTH), BF16), shape((2, WIDTH), F32)),
            in_specs=[vmem] * 3,
            out_specs=(vmem, vmem),
            compiler_params=params,
        )(mine, other, initial)

    def gather(sent):
        mine = lax.all_to_all(sent, "z", 0, 0, tiled=True)
        return mine, lax.ppermute(mine, "core", swap)

    def product(with_rows, mine, other):
        return pl.pallas_call(
            functools.partial(product_kernel, with_rows),
            out_shape=shape((PEERS, SIDE + EXTRA, WIDTH), BF16),
            in_specs=[smem] * 4 + [vmem] * 3,
            out_specs=vmem,
            scratch_shapes=[pltpu.VMEM((PEERS, SIDE, 2 * WIDTH if with_rows else WIDTH), F32)],
            compiler_params=params,
        )(core_at, tile_rows, tile_cols, live_count, tile_values, mine, other)

    with jax.named_scope("gather_one"):
        mine, other = gather(sent)
    with jax.named_scope("product_one"):
        partial_value = product(True, mine, other)
    with jax.named_scope("reduce_one"):
        arrived = lax.all_to_all(partial_value, ("x", "y"), 0, 0, tiled=True)
    with jax.named_scope("middle"):
        sent, row_scale = pl.pallas_call(
            middle_kernel,
            out_shape=(shape((ZS, SIDE + EXTRA, WIDTH), BF16), shape((2, WIDTH), F32)),
            in_specs=[vmem] * 2,
            out_specs=(vmem, vmem),
            compiler_params=params,
        )(arrived, col_scale)
    with jax.named_scope("gather_two"):
        mine, other = gather(sent)
    with jax.named_scope("product_two"):
        partial_value = product(False, mine, other)
    with jax.named_scope("reduce_two"):
        arrived = lax.all_to_all(partial_value, ("x", "y"), 0, 0, tiled=True)
    with jax.named_scope("last"):
        fresh, gram_part, first_piece = pl.pallas_call(
            last_kernel,
            out_shape=(shape((SIDE, WIDTH), F32), shape((WIDTH, WIDTH), F32), shape((8, WIDTH), F32)),
            in_specs=[vmem] * 2,
            out_specs=(vmem,) * 3,
            compiler_params=params,
        )(arrived, row_scale)
    with jax.named_scope("gram"):
        plane = ("core", "x", "y")
        count = 2 * PEERS
        deep = WIDTH // count
        piece = jnp.sum(
            lax.all_to_all(gram_part.reshape(count, deep, WIDTH), plane, 0, 0, tiled=True), axis=0
        )
        both = jnp.concatenate([first_piece, piece], axis=0)
        spread = jnp.broadcast_to(both[None], (ZS, 8 + deep, WIDTH))
        arrived = lax.all_to_all(spread, "z", 0, 0, tiled=True)
        first_gram = arrived[:, :8].reshape(WIDTH, WIDTH)
        piece = jnp.sum(arrived[:, 8:], axis=0)
        spread = jnp.broadcast_to(piece[None], (count, deep, WIDTH))
        gram = lax.all_to_all(spread, plane, 0, 0, tiled=True).reshape(WIDTH, WIDTH)
    with jax.named_scope("finish"):
        return pl.pallas_call(
            finish_kernel,
            out_shape=shape((SIDE, WIDTH), F32),
            in_specs=[vmem] * 3,
            out_specs=vmem,
            compiler_params=params,
        )(first_gram, gram, fresh)


def solution(mesh):
    devices = np.asarray(mesh.devices).reshape(ZS, 2, 4, 4)
    fine = Mesh(devices, ("z", "core", "x", "y"))
    whole = ("z", "core", "x", "y")
    in_specs = (P(whole, None, None), P(whole), P(whole), P(whole), P(whole, None))
    return jax.shard_map(
        shards, mesh=fine, in_specs=in_specs, out_specs=P(whole, None), check_vma=False
    )
```

```python
import functools

import jax
import jax.numpy as jnp
import numpy as np
from jax import lax
from jax.experimental import pallas as pl
from jax.experimental.pallas import tpu as pltpu
from jax.sharding import Mesh, PartitionSpec as P

ZS = 16
PEERS = 16
SIDE = 256
WIDTH = 128
FIRST = 16
SLOTS = 32
GROUP = 16
EXTRA = 16
GRAM_ROWS = 4
VMEM_BYTES = 24 * 1024 * 1024
F32 = jnp.float32
BF16 = jnp.bfloat16
HIGHEST = lax.Precision.HIGHEST

params = pltpu.CompilerParams(vmem_limit_bytes=VMEM_BYTES)
smem = pl.BlockSpec(memory_space=pltpu.SMEM)
vmem = pl.BlockSpec(memory_space=pltpu.VMEM)


def eye_mask():
    return lax.broadcasted_iota(jnp.int32, (WIDTH, WIDTH), 0) == lax.broadcasted_iota(
        jnp.int32, (WIDTH, WIDTH), 1
    )


def to_column(lanes):
    spread = jnp.broadcast_to(lanes, (WIDTH, WIDTH))
    return jnp.sum(jnp.where(eye_mask(), spread, 0.0), axis=1, keepdims=True)


def split3(value):
    high = value.astype(BF16)
    rest = value - high.astype(F32)
    middle = rest.astype(BF16)
    low = (rest - middle.astype(F32)).astype(BF16)
    return high, middle, low


def degree_kernel(cols_ref, live_ref, tiles_ref, out_ref, acc_ref):
    acc_ref[...] = jnp.zeros_like(acc_ref)

    def one(slot, carry):
        tile = tiles_ref[slot].astype(F32).reshape(SIDE // 8, 8, SIDE)
        acc_ref[cols_ref[slot]] += jnp.sum(tile, axis=0)
        return carry

    lax.fori_loop(0, live_ref[0], one, 0)
    out_ref[...] = jnp.zeros_like(out_ref)
    for block in range(2 * ZS):
        total = jnp.sum(acc_ref[block], axis=0, keepdims=True)
        at = 2 * (block % 2)
        out_ref[block // 2, at : at + 1, :] = total[:, :WIDTH]
        out_ref[block // 2, at + 1 : at + 2, :] = total[:, WIDTH:]


def scale_kernel(mine_ref, other_ref, initial_ref, out_ref, scale_ref):
    degree = mine_ref[...] + other_ref[...]
    scale = lax.rsqrt(degree)
    scale_ref[...] = scale
    for half in range(2):
        rows = slice(half * WIDTH, (half + 1) * WIDTH)
        column = to_column(scale[half : half + 1])
        out_ref[rows] = (column * initial_ref[rows].astype(F32)).astype(BF16)


def product_kernel(with_rows, place_ref, rows_ref, cols_ref, live_ref, tiles_ref, *refs):
    *parts, out_ref, acc_ref = refs
    live = live_ref[0]

    def product(slot):
        col = cols_ref[slot]
        core, level = lax.rem(col, 2), lax.div(col, 2)
        odd, at = lax.rem(level, 2), lax.div(level, 2)
        same_core, same_odd = core == place_ref[0], odd == place_ref[1]
        near = jnp.where(same_odd, parts[0][at], parts[1][at])
        far = jnp.where(same_odd, parts[2][at], parts[3][at])
        block = jnp.where(same_core, near, far)
        if with_rows:
            block = jnp.concatenate([block, jnp.ones((SIDE, WIDTH), BF16)], axis=1)
        block = jnp.where(slot < live, block, jnp.zeros_like(block))
        return jnp.dot(tiles_ref[slot], block, preferred_element_type=F32)

    def first(turn, carry):
        slots = [turn * GROUP + at for at in range(GROUP)]
        for slot, value in zip(slots, [product(slot) for slot in slots]):
            acc_ref[rows_ref[slot]] = value
        return carry

    def later(turn, carry):
        slots = [turn * GROUP + at for at in range(GROUP)]
        for slot, value in zip(slots, [product(slot) for slot in slots]):
            acc_ref[rows_ref[slot]] += value
        return carry

    lax.fori_loop(0, FIRST // GROUP, first, 0)
    lax.fori_loop(FIRST // GROUP, SLOTS // GROUP, later, 0)
    if with_rows:
        eye = eye_mask()
        zero = jnp.zeros((EXTRA - 6, WIDTH), BF16)
        for block in range(PEERS):
            out_ref[block, :SIDE] = acc_ref[block, :, :WIDTH].astype(BF16)
            pieces = []
            for half in range(2):
                spread = acc_ref[block, half * WIDTH : (half + 1) * WIDTH, WIDTH:]
                pieces.append(jnp.sum(jnp.where(eye, spread, 0.0), axis=0, keepdims=True))
            three = split3(jnp.concatenate(pieces, axis=0))
            out_ref[block, SIDE:] = jnp.concatenate(list(three) + [zero], axis=0)
    else:
        for block in range(PEERS):
            out_ref[block] = acc_ref[block].astype(BF16)


def total_of(ref, rows):
    total = ref[0, rows].astype(F32)
    for peer in range(1, PEERS):
        total += ref[peer, rows].astype(F32)
    return total


def gram_of(fresh):
    return lax.dot_general(
        fresh, fresh, (((0,), (0,)), ((), ())), precision=HIGHEST, preferred_element_type=F32
    )


def middle_kernel(arrived_ref, col_scale_ref, out_ref, row_scale_ref, gram_ref):
    extra = total_of(arrived_ref, slice(SIDE, SIDE + EXTRA))
    degree = extra[0:2] + extra[2:4] + extra[4:6]
    row_scale = lax.rsqrt(degree)
    row_scale_ref[...] = row_scale
    halves = []
    for half in range(2):
        rows = slice(half * WIDTH, (half + 1) * WIDTH)
        fresh = to_column(row_scale[half : half + 1]) * total_of(arrived_ref, rows)
        halves.append(fresh)
        out_ref[rows] = (to_column(col_scale_ref[half : half + 1]) * fresh).astype(BF16)
    gram_ref[...] = gram_of(jnp.concatenate(halves, axis=0))


def last_kernel(arrived_ref, row_scale_ref, first_gram_ref, fresh_ref, out_ref):
    halves = []
    for half in range(2):
        rows = slice(half * WIDTH, (half + 1) * WIDTH)
        fresh = to_column(row_scale_ref[half : half + 1]) * total_of(arrived_ref, rows)
        fresh_ref[rows] = fresh
        halves.append(fresh)
    gram = gram_of(jnp.concatenate(halves, axis=0))
    for peer in range(2 * PEERS):
        rows = slice(GRAM_ROWS * peer, GRAM_ROWS * (peer + 1))
        out_ref[peer, :GRAM_ROWS] = first_gram_ref[rows]
        out_ref[peer, GRAM_ROWS:] = gram[rows]


def lower_inverse(matrix):
    groups = WIDTH // 8
    parts = [matrix[8 * g : 8 * g + 8] for g in range(groups)]
    lane = lax.broadcasted_iota(jnp.int32, (8, WIDTH), 1)
    row = lax.broadcasted_iota(jnp.int32, (8, WIDTH), 0)
    out = []
    for g in range(groups):
        at = 8 * g
        panel = parts[g]
        inside = (lane >= at) & (lane < at + 8)
        cols = [jnp.broadcast_to(panel[:, at + j : at + j + 1], (8, WIDTH)) for j in range(8)]
        left = {}
        rows = []
        for i in range(8):
            for j in range(i + 1):
                left[i, j] = jnp.broadcast_to(cols[j][i : i + 1], (8, WIDTH))
            unit = jnp.where(lane == at + i, 1.0, 0.0)
            rows.append(jnp.where(inside, unit, jnp.broadcast_to(panel[i : i + 1], (8, WIDTH))))
        inverse, lower = [], {}
        for p in range(8):
            inverse.append(1.0 / left[p, p])
            for i in range(p + 1, 8):
                lower[i, p] = left[i, p] * inverse[p]
            for i in range(p + 1, 8):
                for j in range(p + 1, i + 1):
                    left[i, j] = left[i, j] - lower[i, p] * left[j, p]
                rows[i] = rows[i] - lower[i, p] * rows[p]
        total = jnp.zeros((8, WIDTH), F32)
        for i in range(8):
            total = jnp.where(row == i, rows[i] * lax.rsqrt(left[i, i]), total)
        out.append(jnp.where(lane <= row + at, total, 0.0))
        solved = {}
        for i in reversed(range(8)):
            solved[i] = rows[i] * inverse[i]
            for j in range(7, i, -1):
                solved[i] = solved[i] - lower[j, i] * solved[j]
        for h in range(g + 1, groups):
            even, odd = jnp.where(inside, 0.0, parts[h]), jnp.zeros((8, WIDTH), F32)
            for j in range(8):
                term = jnp.broadcast_to(parts[h][:, at + j : at + j + 1], (8, WIDTH)) * solved[j]
                if j % 2 == 0:
                    even = even - term
                else:
                    odd = odd + term
            parts[h] = even - odd
    return jnp.concatenate(out, axis=0)


def dot(a, b, dims):
    return lax.dot_general(a, b, (dims, ((), ())), precision=HIGHEST, preferred_element_type=F32)


def finish_kernel(grams_ref, fresh_ref, out_ref):
    first_gram = grams_ref[:, :GRAM_ROWS].reshape(WIDTH, WIDTH)
    gram = grams_ref[:, GRAM_ROWS:].reshape(WIDTH, WIDTH)
    first = lower_inverse(first_gram)
    gram = dot(dot(first, gram, ((1,), (0,))), first, ((1,), (1,)))
    second = lower_inverse(gram)
    fresh = dot(fresh_ref[...], first, ((1,), (1,)))
    out_ref[...] = dot(fresh, second, ((1,), (1,)))


def shape(dims, dtype):
    return jax.ShapeDtypeStruct(dims, dtype)


def shards(tile_values, tile_rows, tile_cols, live_count, initial):
    core = lax.axis_index("core")
    odd = lax.axis_index("odd")
    place = jnp.stack([core, odd]).astype(jnp.int32)
    levels = ("level", "odd")
    plane = ("core", "x", "y")
    swap = [(0, 1), (1, 0)]

    with jax.named_scope("col_degree"):
        part = pl.pallas_call(
            degree_kernel,
            out_shape=shape((ZS, 8, WIDTH), F32),
            in_specs=[smem, smem, vmem],
            out_specs=vmem,
            scratch_shapes=[pltpu.VMEM((2 * ZS, 8, SIDE), F32)],
            compiler_params=params,
        )(tile_cols, live_count, tile_values)
        pieces = jnp.sum(lax.all_to_all(part, levels, 0, 0, tiled=True), axis=0)
        mine = lax.dynamic_slice_in_dim(pieces, 2 * core, 2, 0)
        other = lax.ppermute(lax.dynamic_slice_in_dim(pieces, 2 - 2 * core, 2, 0), "core", swap)
    with jax.named_scope("scale"):
        sent, col_scale = pl.pallas_call(
            scale_kernel,
            out_shape=(shape((SIDE, WIDTH), BF16), shape((2, WIDTH), F32)),
            in_specs=[vmem] * 3,
            out_specs=(vmem, vmem),
            compiler_params=params,
        )(mine, other, initial)

    def gather(sent):
        mine = lax.all_gather(sent, "level", axis=0)
        beside = lax.ppermute(mine, "odd", swap)
        return mine, beside, lax.ppermute(mine, "core", swap), lax.ppermute(beside, "core", swap)

    def product(with_rows, parts):
        extra, width = (EXTRA, 2 * WIDTH) if with_rows else (0, WIDTH)
        return pl.pallas_call(
            functools.partial(product_kernel, with_rows),
            out_shape=shape((PEERS, SIDE + extra, WIDTH), BF16),
            in_specs=[smem] * 4 + [vmem] * 5,
            out_specs=vmem,
            scratch_shapes=[pltpu.VMEM((PEERS, SIDE, width), F32)],
            compiler_params=params,
        )(place, tile_rows, tile_cols, live_count, tile_values, *parts)

    with jax.named_scope("gather_one"):
        parts = gather(sent)
    with jax.named_scope("product_one"):
        partial_value = product(True, parts)
    with jax.named_scope("reduce_one"):
        arrived = lax.all_to_all(partial_value, ("x", "y"), 0, 0, tiled=True)
    with jax.named_scope("middle"):
        sent, row_scale, first_gram = pl.pallas_call(
            middle_kernel,
            out_shape=(shape((SIDE, WIDTH), BF16), shape((2, WIDTH), F32), shape((WIDTH, WIDTH), F32)),
            in_specs=[vmem] * 2,
            out_specs=(vmem,) * 3,
            compiler_params=params,
        )(arrived, col_scale)
    with jax.named_scope("gather_two"):
        parts = gather(sent)
    with jax.named_scope("product_two"):
        partial_value = product(False, parts)
    with jax.named_scope("reduce_two"):
        arrived = lax.all_to_all(partial_value, ("x", "y"), 0, 0, tiled=True)
    with jax.named_scope("last"):
        count, deep = 2 * PEERS, 2 * GRAM_ROWS
        fresh, grams = pl.pallas_call(
            last_kernel,
            out_shape=(shape((SIDE, WIDTH), F32), shape((count, deep, WIDTH), F32)),
            in_specs=[vmem] * 3,
            out_specs=(vmem,) * 2,
            compiler_params=params,
        )(arrived, row_scale, first_gram)
    with jax.named_scope("gram"):
        piece = jnp.sum(lax.all_to_all(grams, plane, 0, 0, tiled=True), axis=0)
        spread = jnp.broadcast_to(piece[None], (ZS, deep, WIDTH))
        piece = jnp.sum(lax.all_to_all(spread, levels, 0, 0, tiled=True), axis=0)
        spread = jnp.broadcast_to(piece[None], (count, deep, WIDTH))
        grams = lax.all_to_all(spread, plane, 0, 0, tiled=True)
    with jax.named_scope("finish"):
        return pl.pallas_call(
            finish_kernel,
            out_shape=shape((SIDE, WIDTH), F32),
            in_specs=[vmem] * 2,
            out_specs=vmem,
            compiler_params=params,
        )(grams, fresh)


def solution(mesh):
    devices = np.asarray(mesh.devices).reshape(ZS // 2, 2, 2, 4, 4)
    whole = ("level", "odd", "core", "x", "y")
    fine = Mesh(devices, whole)
    in_specs = (P(whole, None, None), P(whole), P(whole), P(whole), P(whole, None))
    return jax.shard_map(
        shards, mesh=fine, in_specs=in_specs, out_specs=P(whole, None), check_vma=False
    )
```

```python
import functools

import jax
import jax.numpy as jnp
import numpy as np
from jax import lax
from jax.experimental import pallas as pl
from jax.experimental.pallas import tpu as pltpu
from jax.sharding import Mesh, PartitionSpec as P

ZS = 16
QUADS = 4
PEERS = 16
SIDE = 256
WIDTH = 128
SLOTS = 32
GROUP = 16
DEGREE_PARTS = 4
EXTRA = 16
GRAM_ROWS = 4
VMEM_BYTES = 24 * 1024 * 1024
F32 = jnp.float32
BF16 = jnp.bfloat16
HIGHEST = lax.Precision.HIGHEST

params = pltpu.CompilerParams(vmem_limit_bytes=VMEM_BYTES)
degree_params = pltpu.CompilerParams(vmem_limit_bytes=61 * 1024 * 1024)
product_params = pltpu.CompilerParams(vmem_limit_bytes=48 * 1024 * 1024)
smem = pl.BlockSpec(memory_space=pltpu.SMEM)
vmem = pl.BlockSpec(memory_space=pltpu.VMEM)
hbm = pl.BlockSpec(memory_space=pl.ANY)


def eye_mask():
    return lax.broadcasted_iota(jnp.int32, (WIDTH, WIDTH), 0) == lax.broadcasted_iota(
        jnp.int32, (WIDTH, WIDTH), 1
    )


def to_column(lanes):
    spread = jnp.broadcast_to(lanes, (WIDTH, WIDTH))
    return jnp.sum(jnp.where(eye_mask(), spread, 0.0), axis=1, keepdims=True)


def split3(value):
    high = value.astype(BF16)
    rest = value - high.astype(F32)
    middle = rest.astype(BF16)
    low = (rest - middle.astype(F32)).astype(BF16)
    return high, middle, low


def tile_copies(parts, tiles_ref, held_ref, sems):
    size = SLOTS // parts
    copies = []
    for part in range(parts):
        rows = pl.ds(part * size, size)
        copies.append(pltpu.make_async_copy(tiles_ref.at[rows], held_ref.at[rows], sems.at[part]))
    return copies


def degree_kernel(cols_ref, live_ref, tiles_ref, out_ref, held_ref, acc_ref, sems):
    copies = tile_copies(DEGREE_PARTS, tiles_ref, held_ref, sems)
    for copy in copies:
        copy.start()
    acc_ref[...] = jnp.zeros_like(acc_ref)
    size = SLOTS // DEGREE_PARTS

    def one(slot, carry):
        @pl.when(slot < live_ref[0])
        def _():
            tile = held_ref[slot].astype(F32).reshape(SIDE // 8, 8, SIDE)
            acc_ref[cols_ref[slot]] += jnp.sum(tile, axis=0)

        return carry

    for part, copy in enumerate(copies):
        copy.wait()
        lax.fori_loop(part * size, part * size + size, one, 0)
    out_ref[...] = jnp.zeros_like(out_ref)
    for block in range(2 * ZS):
        total = jnp.sum(acc_ref[block], axis=0, keepdims=True)
        at = 2 * (block % 2)
        out_ref[block // 2, at : at + 1, :] = total[:, :WIDTH]
        out_ref[block // 2, at + 1 : at + 2, :] = total[:, WIDTH:]


def scale_kernel(place_ref, pieces_ref, initial_ref, out_ref, scale_ref):
    both = pieces_ref[0] + pieces_ref[1]
    scale = lax.rsqrt(jnp.where(place_ref[0] == 0, both[0:2], both[2:4]))
    scale_ref[...] = scale
    for half in range(2):
        rows = slice(half * WIDTH, (half + 1) * WIDTH)
        column = to_column(scale[half : half + 1])
        out_ref[rows] = (column * initial_ref[rows].astype(F32)).astype(BF16)


def product_kernel(with_rows, place_ref, rows_ref, cols_ref, live_ref, tiles_ref, near_ref, far_ref, out_ref, acc_ref, *held):
    live = live_ref[0]
    if with_rows:
        held_ref, sems = held
        copies = tile_copies(SLOTS // GROUP, tiles_ref, held_ref, sems)
        for copy in copies:
            copy.start()
    else:
        held_ref, copies = tiles_ref, []

    def product(slot):
        col = cols_ref[slot]
        core, level = lax.rem(col, 2), lax.div(col, 2)
        at = QUADS * lax.rem(level + QUADS - place_ref[1], QUADS) + lax.div(level, QUADS)
        block = jnp.where(core == place_ref[0], near_ref[at], far_ref[at])
        if with_rows:
            block = jnp.concatenate([block, jnp.ones((SIDE, WIDTH), BF16)], axis=1)
        block = jnp.where(slot < live, block, jnp.zeros_like(block))
        return jnp.dot(held_ref[slot], block, preferred_element_type=F32)

    for turn in range(SLOTS // GROUP):
        if copies:
            copies[turn].wait()
        slots = range(turn * GROUP, (turn + 1) * GROUP)
        for slot, value in zip(slots, [product(slot) for slot in slots]):
            if turn == 0:
                acc_ref[rows_ref[slot]] = value
            else:
                acc_ref[rows_ref[slot]] += value
    if with_rows:
        eye = eye_mask()
        zero = jnp.zeros((EXTRA - 6, WIDTH), BF16)
        for block in range(PEERS):
            out_ref[block, :SIDE] = acc_ref[block, :, :WIDTH].astype(BF16)
            pieces = []
            for half in range(2):
                spread = acc_ref[block, half * WIDTH : (half + 1) * WIDTH, WIDTH:]
                pieces.append(jnp.sum(jnp.where(eye, spread, 0.0), axis=0, keepdims=True))
            three = split3(jnp.concatenate(pieces, axis=0))
            out_ref[block, SIDE:] = jnp.concatenate(list(three) + [zero], axis=0)
    else:
        for block in range(PEERS):
            out_ref[block] = acc_ref[block].astype(BF16)


def total_of(ref, rows):
    total = ref[0, rows].astype(F32)
    for peer in range(1, PEERS):
        total += ref[peer, rows].astype(F32)
    return total


def gram_of(fresh):
    return lax.dot_general(
        fresh, fresh, (((0,), (0,)), ((), ())), precision=HIGHEST, preferred_element_type=F32
    )


def middle_kernel(arrived_ref, col_scale_ref, out_ref, row_scale_ref, gram_ref):
    extra = total_of(arrived_ref, slice(SIDE, SIDE + EXTRA))
    degree = extra[0:2] + extra[2:4] + extra[4:6]
    row_scale = lax.rsqrt(degree)
    row_scale_ref[...] = row_scale
    halves = []
    for half in range(2):
        rows = slice(half * WIDTH, (half + 1) * WIDTH)
        fresh = to_column(row_scale[half : half + 1]) * total_of(arrived_ref, rows)
        halves.append(fresh)
        out_ref[rows] = (to_column(col_scale_ref[half : half + 1]) * fresh).astype(BF16)
    gram_ref[...] = gram_of(jnp.concatenate(halves, axis=0))


def last_kernel(arrived_ref, row_scale_ref, first_gram_ref, fresh_ref, out_ref):
    halves = []
    for half in range(2):
        rows = slice(half * WIDTH, (half + 1) * WIDTH)
        fresh = to_column(row_scale_ref[half : half + 1]) * total_of(arrived_ref, rows)
        fresh_ref[rows] = fresh
        halves.append(fresh)
    gram = gram_of(jnp.concatenate(halves, axis=0))
    for peer in range(2 * PEERS):
        rows = slice(GRAM_ROWS * peer, GRAM_ROWS * (peer + 1))
        out_ref[peer, :GRAM_ROWS] = first_gram_ref[rows]
        out_ref[peer, GRAM_ROWS:] = gram[rows]


def lower_inverse(matrix):
    groups = WIDTH // 8
    parts = [matrix[8 * g : 8 * g + 8] for g in range(groups)]
    lane = lax.broadcasted_iota(jnp.int32, (8, WIDTH), 1)
    row = lax.broadcasted_iota(jnp.int32, (8, WIDTH), 0)
    out = []
    for g in range(groups):
        at = 8 * g
        panel = parts[g]
        inside = (lane >= at) & (lane < at + 8)
        cols = [jnp.broadcast_to(panel[:, at + j : at + j + 1], (8, WIDTH)) for j in range(8)]
        left = {}
        rows = []
        for i in range(8):
            for j in range(i + 1):
                left[i, j] = jnp.broadcast_to(cols[j][i : i + 1], (8, WIDTH))
            unit = jnp.where(lane == at + i, 1.0, 0.0)
            rows.append(jnp.where(inside, unit, jnp.broadcast_to(panel[i : i + 1], (8, WIDTH))))
        inverse, lower = [], {}
        for p in range(8):
            inverse.append(1.0 / left[p, p])
            for i in range(p + 1, 8):
                lower[i, p] = left[i, p] * inverse[p]
            for i in range(p + 1, 8):
                for j in range(p + 1, i + 1):
                    left[i, j] = left[i, j] - lower[i, p] * left[j, p]
                rows[i] = rows[i] - lower[i, p] * rows[p]
        total = jnp.zeros((8, WIDTH), F32)
        for i in range(8):
            total = jnp.where(row == i, rows[i] * lax.rsqrt(left[i, i]), total)
        out.append(jnp.where(lane <= row + at, total, 0.0))
        solved = {}
        for i in reversed(range(8)):
            solved[i] = rows[i] * inverse[i]
            for j in range(7, i, -1):
                solved[i] = solved[i] - lower[j, i] * solved[j]
        for h in range(g + 1, groups):
            even, odd = jnp.where(inside, 0.0, parts[h]), jnp.zeros((8, WIDTH), F32)
            for j in range(8):
                term = jnp.broadcast_to(parts[h][:, at + j : at + j + 1], (8, WIDTH)) * solved[j]
                if j % 2 == 0:
                    even = even - term
                else:
                    odd = odd + term
            parts[h] = even - odd
    return jnp.concatenate(out, axis=0)


def dot(a, b, dims):
    return lax.dot_general(a, b, (dims, ((), ())), precision=HIGHEST, preferred_element_type=F32)


def finish_kernel(grams_ref, fresh_ref, out_ref):
    first_gram = grams_ref[:, :GRAM_ROWS].reshape(WIDTH, WIDTH)
    gram = grams_ref[:, GRAM_ROWS:].reshape(WIDTH, WIDTH)
    first = lower_inverse(first_gram)
    gram = dot(dot(first, gram, ((1,), (0,))), first, ((1,), (1,)))
    second = lower_inverse(gram)
    fresh = dot(fresh_ref[...], first, ((1,), (1,)))
    out_ref[...] = dot(fresh, second, ((1,), (1,)))


def shape(dims, dtype):
    return jax.ShapeDtypeStruct(dims, dtype)


def shards(tile_values, tile_rows, tile_cols, live_count, initial):
    core = lax.axis_index("core")
    place = jnp.stack([core, lax.axis_index("spot")]).astype(jnp.int32)
    levels = ("quad", "spot")
    plane = ("core", "x", "y")

    with jax.named_scope("col_degree"):
        part = pl.pallas_call(
            degree_kernel,
            out_shape=shape((ZS, 8, WIDTH), F32),
            in_specs=[smem, smem, hbm],
            out_specs=vmem,
            scratch_shapes=[
                pltpu.VMEM(tile_values.shape, BF16),
                pltpu.VMEM((2 * ZS, 8, SIDE), F32),
                pltpu.SemaphoreType.DMA((DEGREE_PARTS,)),
            ],
            compiler_params=degree_params,
        )(tile_cols, live_count, tile_values)
        pieces = jnp.sum(lax.all_to_all(part, levels, 0, 0, tiled=True), axis=0)
        pieces = lax.all_gather(pieces, "core", axis=0)
    with jax.named_scope("scale"):
        sent, col_scale = pl.pallas_call(
            scale_kernel,
            out_shape=(shape((SIDE, WIDTH), BF16), shape((2, WIDTH), F32)),
            in_specs=[smem, vmem, vmem],
            out_specs=(vmem, vmem),
            compiler_params=params,
        )(place, pieces, initial)

    def from_level(first, second):
        steps = (first, second)
        return [
            (((z + steps[core]) % ZS) * 2 + core, z * 2 + core) for z in range(ZS) for core in range(2)
        ]

    def gather(sent):
        chips = levels + ("core",)
        mine = lax.all_gather(sent, "quad", axis=0)
        two = lax.ppermute(mine, chips, from_level(2, -2))
        one = lax.ppermute(mine, chips, from_level(1, 1))
        three = lax.ppermute(mine, chips, from_level(-1, -1))
        near = jnp.concatenate([mine, one, two, three], axis=0)
        return near, lax.ppermute(near, "core", [(0, 1), (1, 0)])

    def product(with_rows, parts):
        extra, width = (EXTRA, 2 * WIDTH) if with_rows else (0, WIDTH)
        scratch = [pltpu.VMEM((PEERS, SIDE, width), F32)]
        if with_rows:
            scratch += [pltpu.VMEM(tile_values.shape, BF16), pltpu.SemaphoreType.DMA((SLOTS // GROUP,))]
        return pl.pallas_call(
            functools.partial(product_kernel, with_rows),
            out_shape=shape((PEERS, SIDE + extra, WIDTH), BF16),
            in_specs=[smem] * 4 + [hbm if with_rows else vmem, vmem, vmem],
            out_specs=vmem,
            scratch_shapes=scratch,
            compiler_params=product_params if with_rows else params,
        )(place, tile_rows, tile_cols, live_count, tile_values, *parts)

    with jax.named_scope("gather_one"):
        parts = gather(sent)
    with jax.named_scope("product_one"):
        partial_value = product(True, parts)
    with jax.named_scope("reduce_one"):
        arrived = lax.all_to_all(partial_value, ("x", "y"), 0, 0, tiled=True)
    with jax.named_scope("middle"):
        sent, row_scale, first_gram = pl.pallas_call(
            middle_kernel,
            out_shape=(shape((SIDE, WIDTH), BF16), shape((2, WIDTH), F32), shape((WIDTH, WIDTH), F32)),
            in_specs=[vmem] * 2,
            out_specs=(vmem,) * 3,
            compiler_params=params,
        )(arrived, col_scale)
    with jax.named_scope("gather_two"):
        parts = gather(sent)
    with jax.named_scope("product_two"):
        partial_value = product(False, parts)
    with jax.named_scope("reduce_two"):
        arrived = lax.all_to_all(partial_value, ("x", "y"), 0, 0, tiled=True)
    with jax.named_scope("last"):
        count, deep = 2 * PEERS, 2 * GRAM_ROWS
        fresh, grams = pl.pallas_call(
            last_kernel,
            out_shape=(shape((SIDE, WIDTH), F32), shape((count, deep, WIDTH), F32)),
            in_specs=[vmem] * 3,
            out_specs=(vmem,) * 2,
            compiler_params=params,
        )(arrived, row_scale, first_gram)
    with jax.named_scope("gram"):
        piece = jnp.sum(lax.all_to_all(grams, plane, 0, 0, tiled=True), axis=0)
        spread = jnp.broadcast_to(piece[None], (ZS, deep, WIDTH))
        piece = jnp.sum(lax.all_to_all(spread, levels, 0, 0, tiled=True), axis=0)
        spread = jnp.broadcast_to(piece[None], (count, deep, WIDTH))
        grams = lax.all_to_all(spread, plane, 0, 0, tiled=True)
    with jax.named_scope("finish"):
        return pl.pallas_call(
            finish_kernel,
            out_shape=shape((SIDE, WIDTH), F32),
            in_specs=[vmem] * 2,
            out_specs=vmem,
            compiler_params=params,
        )(grams, fresh)


def solution(mesh):
    devices = np.asarray(mesh.devices).reshape(QUADS, ZS // QUADS, 2, 4, 4)
    whole = ("quad", "spot", "core", "x", "y")
    fine = Mesh(devices, whole)
    in_specs = (P(whole, None, None), P(whole), P(whole), P(whole), P(whole, None))
    return jax.shard_map(
        shards, mesh=fine, in_specs=in_specs, out_specs=P(whole, None), check_vma=False
    )
```

```python
import functools

import jax
import jax.numpy as jnp
import numpy as np
from jax import lax
from jax.experimental import pallas as pl
from jax.experimental.pallas import tpu as pltpu
from jax.sharding import Mesh, PartitionSpec as P

ZS = 16
QUADS = 4
PEERS = 16
SIDE = 256
WIDTH = 128
SLOTS = 32
GROUP = 16
DEGREE_PARTS = 4
EXTRA = 16
GRAM_ROWS = 4
VMEM_BYTES = 24 * 1024 * 1024
F32 = jnp.float32
BF16 = jnp.bfloat16
HIGHEST = lax.Precision.HIGHEST

params = pltpu.CompilerParams(vmem_limit_bytes=VMEM_BYTES)
degree_params = pltpu.CompilerParams(vmem_limit_bytes=61 * 1024 * 1024)
product_params = pltpu.CompilerParams(vmem_limit_bytes=48 * 1024 * 1024)
smem = pl.BlockSpec(memory_space=pltpu.SMEM)
vmem = pl.BlockSpec(memory_space=pltpu.VMEM)
hbm = pl.BlockSpec(memory_space=pl.ANY)


def eye_mask():
    return lax.broadcasted_iota(jnp.int32, (WIDTH, WIDTH), 0) == lax.broadcasted_iota(
        jnp.int32, (WIDTH, WIDTH), 1
    )


def to_column(lanes):
    spread = jnp.broadcast_to(lanes, (WIDTH, WIDTH))
    return jnp.sum(jnp.where(eye_mask(), spread, 0.0), axis=1, keepdims=True)


def split3(value):
    high = value.astype(BF16)
    rest = value - high.astype(F32)
    middle = rest.astype(BF16)
    low = (rest - middle.astype(F32)).astype(BF16)
    return high, middle, low


def tile_copies(parts, tiles_ref, held_ref, sems):
    size = SLOTS // parts
    copies = []
    for part in range(parts):
        rows = pl.ds(part * size, size)
        copies.append(pltpu.make_async_copy(tiles_ref.at[rows], held_ref.at[rows], sems.at[part]))
    return copies


def degree_kernel(cols_ref, live_ref, tiles_ref, initial_ref, out_ref, held_ref, acc_ref, sems):
    copies = tile_copies(DEGREE_PARTS, tiles_ref, held_ref, sems)
    for copy in copies:
        copy.start()
    acc_ref[...] = jnp.zeros_like(acc_ref)
    size = SLOTS // DEGREE_PARTS

    def one(slot, carry):
        @pl.when(slot < live_ref[0])
        def _():
            tile = held_ref[slot].astype(F32).reshape(SIDE // 8, 8, SIDE)
            acc_ref[cols_ref[slot]] += jnp.sum(tile, axis=0)

        return carry

    for part, copy in enumerate(copies):
        copy.wait()
        lax.fori_loop(part * size, part * size + size, one, 0)
    lane = lax.broadcasted_iota(jnp.int32, (1, WIDTH), 1)
    last = jnp.zeros((1, WIDTH), F32)
    for block in range(2 * ZS):
        total = jnp.sum(acc_ref[block], axis=0, keepdims=True)
        at = 2 * (block % 2)
        out_ref[block // 2, at : at + 1, :] = total[:, :WIDTH]
        out_ref[block // 2, at + 1 : at + 2, :] = total[:, WIDTH:]
        last = jnp.where(lane == block, total[:, SIDE - 1 :], last)
    row = initial_ref[SIDE - 16 :].astype(F32)[15:]
    rest = jnp.concatenate([last, row, jnp.zeros((2, WIDTH), F32)], axis=0)
    for peer in range(ZS):
        out_ref[peer, 4:] = rest


def scale_kernel(place_ref, pieces_ref, arrived_ref, initial_ref, out_ref, last_ref, scale_ref):
    both = pieces_ref[0] + pieces_ref[1]
    scale = lax.rsqrt(jnp.where(place_ref[0] == 0, both[0:2], both[2:4]))
    scale_ref[...] = scale
    for half in range(2):
        rows = slice(half * WIDTH, (half + 1) * WIDTH)
        column = to_column(scale[half : half + 1])
        out_ref[rows] = (column * initial_ref[rows].astype(F32)).astype(BF16)
    level = lax.broadcasted_iota(jnp.int32, (ZS, WIDTH), 0)
    lane = lax.broadcasted_iota(jnp.int32, (ZS, WIDTH), 1)
    picked = jnp.where(lane == 2 * level + place_ref[0], jnp.broadcast_to(both[4:5], (ZS, WIDTH)), 0.0)
    degree = jnp.sum(picked, axis=1, keepdims=True)
    last_ref[...] = (lax.rsqrt(degree) * arrived_ref[:, 5, :]).astype(BF16)


def product_kernel(with_rows, place_ref, rows_ref, cols_ref, live_ref, tiles_ref, near_ref, far_ref, out_ref, acc_ref, *held):
    live = live_ref[0]
    if with_rows:
        held_ref, sems = held
        copies = tile_copies(SLOTS // GROUP, tiles_ref, held_ref, sems)
        for copy in copies:
            copy.start()
    else:
        held_ref, copies = tiles_ref, []

    def product(slot):
        col = cols_ref[slot]
        core, level = lax.rem(col, 2), lax.div(col, 2)
        if with_rows:
            at = level
        else:
            at = QUADS * lax.rem(level + QUADS - place_ref[1], QUADS) + lax.div(level, QUADS)
        block = jnp.where(core == place_ref[0], near_ref[at], far_ref[at])
        if with_rows:
            block = jnp.concatenate([block, jnp.ones((SIDE, WIDTH), BF16)], axis=1)
        block = jnp.where(slot < live, block, jnp.zeros_like(block))
        return jnp.dot(held_ref[slot], block, preferred_element_type=F32)

    for turn in range(SLOTS // GROUP):
        if copies:
            copies[turn].wait()
        slots = range(turn * GROUP, (turn + 1) * GROUP)
        for slot, value in zip(slots, [product(slot) for slot in slots]):
            if turn == 0:
                acc_ref[rows_ref[slot]] = value
            else:
                acc_ref[rows_ref[slot]] += value
    if with_rows:
        eye = eye_mask()
        zero = jnp.zeros((EXTRA - 6, WIDTH), BF16)
        for block in range(PEERS):
            out_ref[block, :SIDE] = acc_ref[block, :, :WIDTH].astype(BF16)
            pieces = []
            for half in range(2):
                spread = acc_ref[block, half * WIDTH : (half + 1) * WIDTH, WIDTH:]
                pieces.append(jnp.sum(jnp.where(eye, spread, 0.0), axis=0, keepdims=True))
            three = split3(jnp.concatenate(pieces, axis=0))
            out_ref[block, SIDE:] = jnp.concatenate(list(three) + [zero], axis=0)
    else:
        for block in range(PEERS):
            out_ref[block] = acc_ref[block].astype(BF16)


def total_of(ref, rows):
    total = ref[0, rows].astype(F32)
    for peer in range(1, PEERS):
        total += ref[peer, rows].astype(F32)
    return total


def gram_of(fresh):
    return lax.dot_general(
        fresh, fresh, (((0,), (0,)), ((), ())), precision=HIGHEST, preferred_element_type=F32
    )


def middle_kernel(arrived_ref, col_scale_ref, out_ref, row_scale_ref, gram_ref):
    extra = total_of(arrived_ref, slice(SIDE, SIDE + EXTRA))
    degree = extra[0:2] + extra[2:4] + extra[4:6]
    row_scale = lax.rsqrt(degree)
    row_scale_ref[...] = row_scale
    halves = []
    for half in range(2):
        rows = slice(half * WIDTH, (half + 1) * WIDTH)
        fresh = to_column(row_scale[half : half + 1]) * total_of(arrived_ref, rows)
        halves.append(fresh)
        out_ref[rows] = (to_column(col_scale_ref[half : half + 1]) * fresh).astype(BF16)
    gram_ref[...] = gram_of(jnp.concatenate(halves, axis=0))


def last_kernel(arrived_ref, row_scale_ref, first_gram_ref, fresh_ref, out_ref):
    halves = []
    for half in range(2):
        rows = slice(half * WIDTH, (half + 1) * WIDTH)
        fresh = to_column(row_scale_ref[half : half + 1]) * total_of(arrived_ref, rows)
        fresh_ref[rows] = fresh
        halves.append(fresh)
    gram = gram_of(jnp.concatenate(halves, axis=0))
    for peer in range(2 * PEERS):
        rows = slice(GRAM_ROWS * peer, GRAM_ROWS * (peer + 1))
        out_ref[peer, :GRAM_ROWS] = first_gram_ref[rows]
        out_ref[peer, GRAM_ROWS:] = gram[rows]


def lower_inverse(matrix):
    groups = WIDTH // 8
    parts = [matrix[8 * g : 8 * g + 8] for g in range(groups)]
    lane = lax.broadcasted_iota(jnp.int32, (8, WIDTH), 1)
    row = lax.broadcasted_iota(jnp.int32, (8, WIDTH), 0)
    out = []
    for g in range(groups):
        at = 8 * g
        panel = parts[g]
        inside = (lane >= at) & (lane < at + 8)
        cols = [jnp.broadcast_to(panel[:, at + j : at + j + 1], (8, WIDTH)) for j in range(8)]
        left = {}
        rows = []
        for i in range(8):
            for j in range(i + 1):
                left[i, j] = jnp.broadcast_to(cols[j][i : i + 1], (8, WIDTH))
            unit = jnp.where(lane == at + i, 1.0, 0.0)
            rows.append(jnp.where(inside, unit, jnp.broadcast_to(panel[i : i + 1], (8, WIDTH))))
        inverse, lower = [], {}
        for p in range(0, 8, 2):
            a, b, c = left[p, p], left[p + 1, p], left[p + 1, p + 1]
            scale = 1.0 / (a * c - b * b)
            corner, cross, pivot = c * scale, b * scale, a * scale
            inverse += [1.0 / a, pivot]
            lower[p + 1, p] = b * inverse[p]
            left[p + 1, p + 1] = c - b * lower[p + 1, p]
            for i in range(p + 2, 8):
                first = left[i, p] * corner - left[i, p + 1] * cross
                second = left[i, p + 1] * pivot - left[i, p] * cross
                lower[i, p], lower[i, p + 1] = left[i, p] * inverse[p], second
                for j in range(p + 2, i + 1):
                    left[i, j] = left[i, j] - (first * left[j, p] + second * left[j, p + 1])
                rows[i] = rows[i] - (first * rows[p] + second * rows[p + 1])
            rows[p + 1] = rows[p + 1] - lower[p + 1, p] * rows[p]
        total = jnp.zeros((8, WIDTH), F32)
        for i in range(8):
            total = jnp.where(row == i, rows[i] * lax.rsqrt(left[i, i]), total)
        out.append(jnp.where(lane <= row + at, total, 0.0))
        solved = {}
        for i in reversed(range(8)):
            solved[i] = rows[i] * inverse[i]
            for j in range(7, i, -1):
                solved[i] = solved[i] - lower[j, i] * solved[j]
        for h in range(g + 1, groups):
            even, odd = jnp.where(inside, 0.0, parts[h]), jnp.zeros((8, WIDTH), F32)
            for j in range(8):
                term = jnp.broadcast_to(parts[h][:, at + j : at + j + 1], (8, WIDTH)) * solved[j]
                if j % 2 == 0:
                    even = even - term
                else:
                    odd = odd + term
            parts[h] = even - odd
    return jnp.concatenate(out, axis=0)


def dot(a, b, dims):
    return lax.dot_general(a, b, (dims, ((), ())), precision=HIGHEST, preferred_element_type=F32)


def finish_kernel(grams_ref, fresh_ref, out_ref):
    first_gram = grams_ref[:, :GRAM_ROWS].reshape(WIDTH, WIDTH)
    gram = grams_ref[:, GRAM_ROWS:].reshape(WIDTH, WIDTH)
    first = lower_inverse(first_gram)
    gram = dot(dot(first, gram, ((1,), (0,))), first, ((1,), (1,)))
    second = lower_inverse(gram)
    fresh = dot(fresh_ref[...], first, ((1,), (1,)))
    out_ref[...] = dot(fresh, second, ((1,), (1,)))


def shape(dims, dtype):
    return jax.ShapeDtypeStruct(dims, dtype)


def shards(tile_values, tile_rows, tile_cols, live_count, initial):
    core = lax.axis_index("core")
    place = jnp.stack([core, lax.axis_index("spot")]).astype(jnp.int32)
    levels = ("quad", "spot")
    plane = ("core", "x", "y")
    swap = [(0, 1), (1, 0)]

    with jax.named_scope("col_degree"):
        part = pl.pallas_call(
            degree_kernel,
            out_shape=shape((ZS, 8, WIDTH), F32),
            in_specs=[smem, smem, hbm, vmem],
            out_specs=vmem,
            scratch_shapes=[
                pltpu.VMEM(tile_values.shape, BF16),
                pltpu.VMEM((2 * ZS, 8, SIDE), F32),
                pltpu.SemaphoreType.DMA((DEGREE_PARTS,)),
            ],
            compiler_params=degree_params,
        )(tile_cols, live_count, tile_values, initial)
        degrees = lax.all_to_all(part, levels, 0, 0, tiled=True)
        pieces = lax.all_gather(jnp.sum(degrees, axis=0), "core", axis=0)
    with jax.named_scope("scale"):
        sent, last, col_scale = pl.pallas_call(
            scale_kernel,
            out_shape=(
                shape((SIDE, WIDTH), BF16),
                shape((ZS, WIDTH), BF16),
                shape((2, WIDTH), F32),
            ),
            in_specs=[smem] + [vmem] * 3,
            out_specs=(vmem,) * 3,
            compiler_params=params,
        )(place, pieces, degrees, initial)

    def from_level(first, second):
        steps = (first, second)
        return [
            (((z + steps[core]) % ZS) * 2 + core, z * 2 + core) for z in range(ZS) for core in range(2)
        ]

    def gather(sent):
        chips = levels + ("core",)
        mine = lax.all_gather(sent, "quad", axis=0)
        two = lax.ppermute(mine, chips, from_level(2, -2))
        one = lax.ppermute(mine, chips, from_level(1, 1))
        three = lax.ppermute(mine, chips, from_level(-1, -1))
        near = jnp.concatenate([mine, one, two, three], axis=0)
        return near, lax.ppermute(near, "core", swap)

    def product(with_rows, parts):
        extra, width = (EXTRA, 2 * WIDTH) if with_rows else (0, WIDTH)
        scratch = [pltpu.VMEM((PEERS, SIDE, width), F32)]
        if with_rows:
            scratch += [pltpu.VMEM(tile_values.shape, BF16), pltpu.SemaphoreType.DMA((SLOTS // GROUP,))]
        return pl.pallas_call(
            functools.partial(product_kernel, with_rows),
            out_shape=shape((PEERS, SIDE + extra, WIDTH), BF16),
            in_specs=[smem] * 4 + [hbm if with_rows else vmem, vmem, vmem],
            out_specs=vmem,
            scratch_shapes=scratch,
            compiler_params=product_params if with_rows else params,
        )(place, tile_rows, tile_cols, live_count, tile_values, *parts)

    with jax.named_scope("gather_one"):
        near = lax.all_gather(sent[: SIDE - 1], levels, axis=0)
        near = jnp.concatenate([near, last[:, None]], axis=1)
        parts = near, lax.ppermute(near, "core", swap)
    with jax.named_scope("product_one"):
        partial_value = product(True, parts)
    with jax.named_scope("reduce_one"):
        arrived = lax.all_to_all(partial_value, ("x", "y"), 0, 0, tiled=True)
    with jax.named_scope("middle"):
        sent, row_scale, first_gram = pl.pallas_call(
            middle_kernel,
            out_shape=(shape((SIDE, WIDTH), BF16), shape((2, WIDTH), F32), shape((WIDTH, WIDTH), F32)),
            in_specs=[vmem] * 2,
            out_specs=(vmem,) * 3,
            compiler_params=params,
        )(arrived, col_scale)
    with jax.named_scope("gather_two"):
        parts = gather(sent)
    with jax.named_scope("product_two"):
        partial_value = product(False, parts)
    with jax.named_scope("reduce_two"):
        arrived = lax.all_to_all(partial_value, ("x", "y"), 0, 0, tiled=True)
    with jax.named_scope("last"):
        count, deep = 2 * PEERS, 2 * GRAM_ROWS
        fresh, grams = pl.pallas_call(
            last_kernel,
            out_shape=(shape((SIDE, WIDTH), F32), shape((count, deep, WIDTH), F32)),
            in_specs=[vmem] * 3,
            out_specs=(vmem,) * 2,
            compiler_params=params,
        )(arrived, row_scale, first_gram)
    with jax.named_scope("gram"):
        piece = jnp.sum(lax.all_to_all(grams, plane, 0, 0, tiled=True), axis=0)
        spread = jnp.broadcast_to(piece[None], (ZS, deep, WIDTH))
        piece = jnp.sum(lax.all_to_all(spread, levels, 0, 0, tiled=True), axis=0)
        spread = jnp.broadcast_to(piece[None], (count, deep, WIDTH))
        grams = lax.all_to_all(spread, plane, 0, 0, tiled=True)
    with jax.named_scope("finish"):
        return pl.pallas_call(
            finish_kernel,
            out_shape=shape((SIDE, WIDTH), F32),
            in_specs=[vmem] * 2,
            out_specs=vmem,
            compiler_params=params,
        )(grams, fresh)


def solution(mesh):
    devices = np.asarray(mesh.devices).reshape(QUADS, ZS // QUADS, 2, 4, 4)
    whole = ("quad", "spot", "core", "x", "y")
    fine = Mesh(devices, whole)
    in_specs = (P(whole, None, None), P(whole), P(whole), P(whole), P(whole, None))
    return jax.shard_map(
        shards, mesh=fine, in_specs=in_specs, out_specs=P(whole, None), check_vma=False
    )
```

```python
import functools

import jax
import jax.numpy as jnp
import numpy as np
from jax import lax
from jax.experimental import pallas as pl
from jax.experimental.pallas import tpu as pltpu
from jax.sharding import Mesh, PartitionSpec as P

ZS = 16
QUADS = 4
PEERS = 16
SIDE = 256
WIDTH = 128
SLOTS = 32
GROUP = 16
DEGREE_PARTS = 4
EXTRA = 16
GRAM_ROWS = 4
VMEM_BYTES = 24 * 1024 * 1024
F32 = jnp.float32
BF16 = jnp.bfloat16
HIGHEST = lax.Precision.HIGHEST

params = pltpu.CompilerParams(vmem_limit_bytes=VMEM_BYTES)
degree_params = pltpu.CompilerParams(vmem_limit_bytes=61 * 1024 * 1024)
product_params = pltpu.CompilerParams(vmem_limit_bytes=48 * 1024 * 1024)
smem = pl.BlockSpec(memory_space=pltpu.SMEM)
vmem = pl.BlockSpec(memory_space=pltpu.VMEM)
hbm = pl.BlockSpec(memory_space=pl.ANY)


def eye_mask():
    return lax.broadcasted_iota(jnp.int32, (WIDTH, WIDTH), 0) == lax.broadcasted_iota(
        jnp.int32, (WIDTH, WIDTH), 1
    )


def to_column(lanes):
    spread = jnp.broadcast_to(lanes, (WIDTH, WIDTH))
    return jnp.sum(jnp.where(eye_mask(), spread, 0.0), axis=1, keepdims=True)


def split3(value):
    high = value.astype(BF16)
    rest = value - high.astype(F32)
    middle = rest.astype(BF16)
    low = (rest - middle.astype(F32)).astype(BF16)
    return high, middle, low


def tile_copies(parts, tiles_ref, held_ref, sems):
    size = SLOTS // parts
    copies = []
    for part in range(parts):
        rows = pl.ds(part * size, size)
        copies.append(pltpu.make_async_copy(tiles_ref.at[rows], held_ref.at[rows], sems.at[part]))
    return copies


def degree_kernel(cols_ref, live_ref, tiles_ref, initial_ref, out_ref, held_ref, acc_ref, sems):
    copies = tile_copies(DEGREE_PARTS, tiles_ref, held_ref, sems)
    for copy in copies:
        copy.start()
    acc_ref[...] = jnp.zeros_like(acc_ref)
    size = SLOTS // DEGREE_PARTS

    def one(slot, carry):
        @pl.when(slot < live_ref[0])
        def _():
            tile = held_ref[slot].astype(F32).reshape(SIDE // 8, 8, SIDE)
            acc_ref[cols_ref[slot]] += jnp.sum(tile, axis=0)

        return carry

    for part, copy in enumerate(copies):
        copy.wait()
        lax.fori_loop(part * size, part * size + size, one, 0)
    lane = lax.broadcasted_iota(jnp.int32, (1, WIDTH), 1)
    last = jnp.zeros((1, WIDTH), F32)
    for block in range(2 * ZS):
        total = jnp.sum(acc_ref[block], axis=0, keepdims=True)
        at = 2 * (block % 2)
        out_ref[block // 2, at : at + 1, :] = total[:, :WIDTH]
        out_ref[block // 2, at + 1 : at + 2, :] = total[:, WIDTH:]
        last = jnp.where(lane == block, total[:, SIDE - 1 :], last)
    row = initial_ref[SIDE - 16 :].astype(F32)[15:]
    rest = jnp.concatenate([last, row, jnp.zeros((2, WIDTH), F32)], axis=0)
    for peer in range(ZS):
        out_ref[peer, 4:] = rest


def scale_kernel(place_ref, degrees_ref, initial_ref, out_ref, last_ref, scale_ref):
    both = degrees_ref[0, 0] + degrees_ref[1, 0]
    for level in range(1, ZS):
        both += degrees_ref[0, level] + degrees_ref[1, level]
    scale = lax.rsqrt(jnp.where(place_ref[0] == 0, both[0:2], both[2:4]))
    scale_ref[...] = scale
    for half in range(2):
        rows = slice(half * WIDTH, (half + 1) * WIDTH)
        column = to_column(scale[half : half + 1])
        out_ref[rows] = (column * initial_ref[rows].astype(F32)).astype(BF16)
    level = lax.broadcasted_iota(jnp.int32, (ZS, WIDTH), 0)
    lane = lax.broadcasted_iota(jnp.int32, (ZS, WIDTH), 1)
    core = lax.rem(lax.div(level, QUADS) + place_ref[2], 2)
    picked = jnp.where(lane == 2 * level + core, jnp.broadcast_to(both[4:5], (ZS, WIDTH)), 0.0)
    degree = jnp.sum(picked, axis=1, keepdims=True)
    row = jnp.where(core == 0, degrees_ref[0, :, 5, :], degrees_ref[1, :, 5, :])
    last_ref[...] = (lax.rsqrt(degree) * row).astype(BF16)


def product_kernel(with_rows, place_ref, rows_ref, cols_ref, live_ref, tiles_ref, near_ref, far_ref, out_ref, acc_ref, *held):
    live = live_ref[0]
    if with_rows:
        held_ref, sems = held
        copies = tile_copies(SLOTS // GROUP, tiles_ref, held_ref, sems)
        for copy in copies:
            copy.start()
    else:
        held_ref, copies = tiles_ref, []

    def product(slot):
        col = cols_ref[slot]
        core, level = lax.rem(col, 2), lax.div(col, 2)
        if with_rows:
            at, same = level, lax.rem(core + lax.div(level, QUADS), 2) == place_ref[2]
        else:
            at = QUADS * lax.rem(level + QUADS - place_ref[1], QUADS) + lax.div(level, QUADS)
            same = core == place_ref[0]
        block = jnp.where(same, near_ref[at], far_ref[at])
        if with_rows:
            block = jnp.concatenate([block, jnp.ones((SIDE, WIDTH), BF16)], axis=1)
        block = jnp.where(slot < live, block, jnp.zeros_like(block))
        return jnp.dot(held_ref[slot], block, preferred_element_type=F32)

    for turn in range(SLOTS // GROUP):
        if copies:
            copies[turn].wait()
        slots = range(turn * GROUP, (turn + 1) * GROUP)
        for slot, value in zip(slots, [product(slot) for slot in slots]):
            if turn == 0:
                acc_ref[rows_ref[slot]] = value
            else:
                acc_ref[rows_ref[slot]] += value
    if with_rows:
        eye = eye_mask()
        zero = jnp.zeros((EXTRA - 6, WIDTH), BF16)
        for block in range(PEERS):
            out_ref[block, :SIDE] = acc_ref[block, :, :WIDTH].astype(BF16)
            pieces = []
            for half in range(2):
                spread = acc_ref[block, half * WIDTH : (half + 1) * WIDTH, WIDTH:]
                pieces.append(jnp.sum(jnp.where(eye, spread, 0.0), axis=0, keepdims=True))
            three = split3(jnp.concatenate(pieces, axis=0))
            out_ref[block, SIDE:] = jnp.concatenate(list(three) + [zero], axis=0)
    else:
        for block in range(PEERS):
            out_ref[block] = acc_ref[block].astype(BF16)


def total_of(ref, rows):
    total = ref[0, rows].astype(F32)
    for peer in range(1, PEERS):
        total += ref[peer, rows].astype(F32)
    return total


def gram_of(fresh):
    return lax.dot_general(
        fresh, fresh, (((0,), (0,)), ((), ())), precision=HIGHEST, preferred_element_type=F32
    )


def middle_kernel(arrived_ref, col_scale_ref, out_ref, row_scale_ref, gram_ref):
    extra = total_of(arrived_ref, slice(SIDE, SIDE + EXTRA))
    degree = extra[0:2] + extra[2:4] + extra[4:6]
    row_scale = lax.rsqrt(degree)
    row_scale_ref[...] = row_scale
    halves = []
    for half in range(2):
        rows = slice(half * WIDTH, (half + 1) * WIDTH)
        fresh = to_column(row_scale[half : half + 1]) * total_of(arrived_ref, rows)
        halves.append(fresh)
        out_ref[rows] = (to_column(col_scale_ref[half : half + 1]) * fresh).astype(BF16)
    gram_ref[...] = gram_of(jnp.concatenate(halves, axis=0))


def last_kernel(arrived_ref, row_scale_ref, first_gram_ref, fresh_ref, out_ref):
    halves = []
    for half in range(2):
        rows = slice(half * WIDTH, (half + 1) * WIDTH)
        fresh = to_column(row_scale_ref[half : half + 1]) * total_of(arrived_ref, rows)
        fresh_ref[rows] = fresh
        halves.append(fresh)
    gram = gram_of(jnp.concatenate(halves, axis=0))
    for peer in range(2 * PEERS):
        rows = slice(GRAM_ROWS * peer, GRAM_ROWS * (peer + 1))
        out_ref[peer, :GRAM_ROWS] = first_gram_ref[rows]
        out_ref[peer, GRAM_ROWS:] = gram[rows]


def lower_inverse(matrix):
    groups = WIDTH // 8
    parts = [matrix[8 * g : 8 * g + 8] for g in range(groups)]
    lane = lax.broadcasted_iota(jnp.int32, (8, WIDTH), 1)
    row = lax.broadcasted_iota(jnp.int32, (8, WIDTH), 0)
    out = []
    for g in range(groups):
        at = 8 * g
        panel = parts[g]
        inside = (lane >= at) & (lane < at + 8)
        cols = [jnp.broadcast_to(panel[:, at + j : at + j + 1], (8, WIDTH)) for j in range(8)]
        left = {}
        rows = []
        for i in range(8):
            for j in range(i + 1):
                left[i, j] = jnp.broadcast_to(cols[j][i : i + 1], (8, WIDTH))
            unit = jnp.where(lane == at + i, 1.0, 0.0)
            rows.append(jnp.where(inside, unit, jnp.broadcast_to(panel[i : i + 1], (8, WIDTH))))
        inverse, lower = [], {}
        for p in range(0, 8, 2):
            a, b, c = left[p, p], left[p + 1, p], left[p + 1, p + 1]
            scale = 1.0 / (a * c - b * b)
            corner, cross, pivot = c * scale, b * scale, a * scale
            inverse += [1.0 / a, pivot]
            lower[p + 1, p] = b * inverse[p]
            left[p + 1, p + 1] = c - b * lower[p + 1, p]
            for i in range(p + 2, 8):
                first = left[i, p] * corner - left[i, p + 1] * cross
                second = left[i, p + 1] * pivot - left[i, p] * cross
                lower[i, p], lower[i, p + 1] = left[i, p] * inverse[p], second
                for j in range(p + 2, i + 1):
                    left[i, j] = left[i, j] - (first * left[j, p] + second * left[j, p + 1])
                rows[i] = rows[i] - (first * rows[p] + second * rows[p + 1])
            rows[p + 1] = rows[p + 1] - lower[p + 1, p] * rows[p]
        total = jnp.zeros((8, WIDTH), F32)
        for i in range(8):
            total = jnp.where(row == i, rows[i] * lax.rsqrt(left[i, i]), total)
        out.append(jnp.where(lane <= row + at, total, 0.0))
        solved = {}
        for i in reversed(range(8)):
            solved[i] = rows[i] * inverse[i]
            for j in range(7, i, -1):
                solved[i] = solved[i] - lower[j, i] * solved[j]
        for h in range(g + 1, groups):
            even, odd = jnp.where(inside, 0.0, parts[h]), jnp.zeros((8, WIDTH), F32)
            for j in range(8):
                term = jnp.broadcast_to(parts[h][:, at + j : at + j + 1], (8, WIDTH)) * solved[j]
                if j % 2 == 0:
                    even = even - term
                else:
                    odd = odd + term
            parts[h] = even - odd
    return jnp.concatenate(out, axis=0)


def dot(a, b, dims):
    return lax.dot_general(a, b, (dims, ((), ())), precision=HIGHEST, preferred_element_type=F32)


def finish_kernel(grams_ref, fresh_ref, out_ref):
    first_gram = grams_ref[:, :GRAM_ROWS].reshape(WIDTH, WIDTH)
    gram = grams_ref[:, GRAM_ROWS:].reshape(WIDTH, WIDTH)
    first = lower_inverse(first_gram)
    gram = dot(dot(first, gram, ((1,), (0,))), first, ((1,), (1,)))
    second = lower_inverse(gram)
    fresh = dot(fresh_ref[...], first, ((1,), (1,)))
    out_ref[...] = dot(fresh, second, ((1,), (1,)))


def shape(dims, dtype):
    return jax.ShapeDtypeStruct(dims, dtype)


def shards(tile_values, tile_rows, tile_cols, live_count, initial):
    core = lax.axis_index("core")
    group = lax.rem(core + lax.axis_index("quad"), 2)
    place = jnp.stack([core, lax.axis_index("spot"), group]).astype(jnp.int32)
    groups = [[2 * z + (at + z // QUADS) % 2 for z in range(ZS)] for at in range(2)]
    levels = ("quad", "spot")
    plane = ("core", "x", "y")
    swap = [(0, 1), (1, 0)]

    with jax.named_scope("col_degree"):
        part = pl.pallas_call(
            degree_kernel,
            out_shape=shape((ZS, 8, WIDTH), F32),
            in_specs=[smem, smem, hbm, vmem],
            out_specs=vmem,
            scratch_shapes=[
                pltpu.VMEM(tile_values.shape, BF16),
                pltpu.VMEM((2 * ZS, 8, SIDE), F32),
                pltpu.SemaphoreType.DMA((DEGREE_PARTS,)),
            ],
            compiler_params=degree_params,
        )(tile_cols, live_count, tile_values, initial)
        degrees = lax.all_to_all(part, levels, 0, 0, tiled=True)
        degrees = lax.all_gather(degrees, "core", axis=0)
    with jax.named_scope("scale"):
        sent, last, col_scale = pl.pallas_call(
            scale_kernel,
            out_shape=(
                shape((SIDE, WIDTH), BF16),
                shape((ZS, WIDTH), BF16),
                shape((2, WIDTH), F32),
            ),
            in_specs=[smem] + [vmem] * 2,
            out_specs=(vmem,) * 3,
            compiler_params=params,
        )(place, degrees, initial)

    def from_level(first, second):
        steps = (first, second)
        return [
            (((z + steps[core]) % ZS) * 2 + core, z * 2 + core) for z in range(ZS) for core in range(2)
        ]

    def gather(sent):
        chips = levels + ("core",)
        mine = lax.all_gather(sent, "quad", axis=0)
        two = lax.ppermute(mine, chips, from_level(2, -2))
        one = lax.ppermute(mine, chips, from_level(1, 1))
        three = lax.ppermute(mine, chips, from_level(-1, -1))
        near = jnp.concatenate([mine, one, two, three], axis=0)
        return near, lax.ppermute(near, "core", swap)

    def product(with_rows, parts):
        extra, width = (EXTRA, 2 * WIDTH) if with_rows else (0, WIDTH)
        scratch = [pltpu.VMEM((PEERS, SIDE, width), F32)]
        if with_rows:
            scratch += [pltpu.VMEM(tile_values.shape, BF16), pltpu.SemaphoreType.DMA((SLOTS // GROUP,))]
        return pl.pallas_call(
            functools.partial(product_kernel, with_rows),
            out_shape=shape((PEERS, SIDE + extra, WIDTH), BF16),
            in_specs=[smem] * 4 + [hbm if with_rows else vmem, vmem, vmem],
            out_specs=vmem,
            scratch_shapes=scratch,
            compiler_params=product_params if with_rows else params,
        )(place, tile_rows, tile_cols, live_count, tile_values, *parts)

    with jax.named_scope("gather_one"):
        near = lax.all_gather(sent[: SIDE - 1], levels + ("core",), axis=0, axis_index_groups=groups)
        near = jnp.concatenate([near, last[:, None]], axis=1)
        parts = near, lax.ppermute(near, "core", swap)
    with jax.named_scope("product_one"):
        partial_value = product(True, parts)
    with jax.named_scope("reduce_one"):
        arrived = lax.all_to_all(partial_value, ("x", "y"), 0, 0, tiled=True)
    with jax.named_scope("middle"):
        sent, row_scale, first_gram = pl.pallas_call(
            middle_kernel,
            out_shape=(shape((SIDE, WIDTH), BF16), shape((2, WIDTH), F32), shape((WIDTH, WIDTH), F32)),
            in_specs=[vmem] * 2,
            out_specs=(vmem,) * 3,
            compiler_params=params,
        )(arrived, col_scale)
    with jax.named_scope("gather_two"):
        parts = gather(sent)
    with jax.named_scope("product_two"):
        partial_value = product(False, parts)
    with jax.named_scope("reduce_two"):
        arrived = lax.all_to_all(partial_value, ("x", "y"), 0, 0, tiled=True)
    with jax.named_scope("last"):
        count, deep = 2 * PEERS, 2 * GRAM_ROWS
        fresh, grams = pl.pallas_call(
            last_kernel,
            out_shape=(shape((SIDE, WIDTH), F32), shape((count, deep, WIDTH), F32)),
            in_specs=[vmem] * 3,
            out_specs=(vmem,) * 2,
            compiler_params=params,
        )(arrived, row_scale, first_gram)
    with jax.named_scope("gram"):
        piece = jnp.sum(lax.all_to_all(grams, plane, 0, 0, tiled=True), axis=0)
        spread = jnp.broadcast_to(piece[None], (ZS, deep, WIDTH))
        piece = jnp.sum(lax.all_to_all(spread, levels, 0, 0, tiled=True), axis=0)
        spread = jnp.broadcast_to(piece[None], (count, deep, WIDTH))
        grams = lax.all_to_all(spread, plane, 0, 0, tiled=True)
    with jax.named_scope("finish"):
        return pl.pallas_call(
            finish_kernel,
            out_shape=shape((SIDE, WIDTH), F32),
            in_specs=[vmem] * 2,
            out_specs=vmem,
            compiler_params=params,
        )(grams, fresh)


def solution(mesh):
    devices = np.asarray(mesh.devices).reshape(QUADS, ZS // QUADS, 2, 4, 4)
    whole = ("quad", "spot", "core", "x", "y")
    fine = Mesh(devices, whole)
    in_specs = (P(whole, None, None), P(whole), P(whole), P(whole), P(whole, None))
    return jax.shard_map(
        shards, mesh=fine, in_specs=in_specs, out_specs=P(whole, None), check_vma=False
    )
```

```python
import functools

import jax
import jax.numpy as jnp
import numpy as np
from jax import lax
from jax.experimental import pallas as pl
from jax.experimental.pallas import tpu as pltpu
from jax.sharding import Mesh, PartitionSpec as P

ZS = 16
QUADS = 4
PEERS = 16
SIDE = 256
WIDTH = 128
SLOTS = 32
GROUP = 16
DEGREE_PARTS = 4
EXTRA = 16
GRAM_ROWS = 4
VMEM_BYTES = 24 * 1024 * 1024
F32 = jnp.float32
BF16 = jnp.bfloat16
HIGHEST = lax.Precision.HIGHEST

params = pltpu.CompilerParams(vmem_limit_bytes=VMEM_BYTES)
degree_params = pltpu.CompilerParams(vmem_limit_bytes=61 * 1024 * 1024)
product_params = pltpu.CompilerParams(vmem_limit_bytes=48 * 1024 * 1024)
smem = pl.BlockSpec(memory_space=pltpu.SMEM)
vmem = pl.BlockSpec(memory_space=pltpu.VMEM)
hbm = pl.BlockSpec(memory_space=pl.ANY)


def eye_mask():
    return lax.broadcasted_iota(jnp.int32, (WIDTH, WIDTH), 0) == lax.broadcasted_iota(
        jnp.int32, (WIDTH, WIDTH), 1
    )


def to_column(lanes):
    spread = jnp.broadcast_to(lanes, (WIDTH, WIDTH))
    return jnp.sum(jnp.where(eye_mask(), spread, 0.0), axis=1, keepdims=True)


def split3(value):
    high = value.astype(BF16)
    rest = value - high.astype(F32)
    middle = rest.astype(BF16)
    low = (rest - middle.astype(F32)).astype(BF16)
    return high, middle, low


def tile_copies(parts, tiles_ref, held_ref, sems):
    size = SLOTS // parts
    copies = []
    for part in range(parts):
        rows = pl.ds(part * size, size)
        copies.append(pltpu.make_async_copy(tiles_ref.at[rows], held_ref.at[rows], sems.at[part]))
    return copies


def degree_kernel(cols_ref, live_ref, tiles_ref, initial_ref, out_ref, held_ref, acc_ref, sems):
    copies = tile_copies(DEGREE_PARTS, tiles_ref, held_ref, sems)
    for copy in copies:
        copy.start()
    acc_ref[...] = jnp.zeros_like(acc_ref)
    size = SLOTS // DEGREE_PARTS

    def one(slot, carry):
        @pl.when(slot < live_ref[0])
        def _():
            tile = held_ref[slot].astype(F32).reshape(SIDE // 8, 8, SIDE)
            acc_ref[cols_ref[slot]] += jnp.sum(tile, axis=0)

        return carry

    for part, copy in enumerate(copies):
        copy.wait()
        lax.fori_loop(part * size, part * size + size, one, 0)
    lane = lax.broadcasted_iota(jnp.int32, (1, WIDTH), 1)
    last = jnp.zeros((1, WIDTH), F32)
    for block in range(2 * ZS):
        total = jnp.sum(acc_ref[block], axis=0, keepdims=True)
        at = 2 * (block % 2)
        out_ref[block // 2, at : at + 1, :] = total[:, :WIDTH]
        out_ref[block // 2, at + 1 : at + 2, :] = total[:, WIDTH:]
        last = jnp.where(lane == block, total[:, SIDE - 1 :], last)
    row = initial_ref[SIDE - 16 :].astype(F32)[15:]
    rest = jnp.concatenate([last, row, jnp.zeros((2, WIDTH), F32)], axis=0)
    for peer in range(ZS):
        out_ref[peer, 4:] = rest


def scale_kernel(place_ref, degrees_ref, initial_ref, out_ref, last_ref, scale_ref):
    both = degrees_ref[0, 0] + degrees_ref[1, 0]
    for level in range(1, ZS):
        both += degrees_ref[0, level] + degrees_ref[1, level]
    scale = lax.rsqrt(jnp.where(place_ref[0] == 0, both[0:2], both[2:4]))
    scale_ref[...] = scale
    for half in range(2):
        rows = slice(half * WIDTH, (half + 1) * WIDTH)
        column = to_column(scale[half : half + 1])
        out_ref[rows] = (column * initial_ref[rows].astype(F32)).astype(BF16)
    level = lax.broadcasted_iota(jnp.int32, (ZS, WIDTH), 0)
    lane = lax.broadcasted_iota(jnp.int32, (ZS, WIDTH), 1)
    core = lax.rem(lax.div(level, QUADS) + place_ref[2], 2)
    picked = jnp.where(lane == 2 * level + core, jnp.broadcast_to(both[4:5], (ZS, WIDTH)), 0.0)
    degree = jnp.sum(picked, axis=1, keepdims=True)
    row = jnp.where(core == 0, degrees_ref[0, :, 5, :], degrees_ref[1, :, 5, :])
    last_ref[...] = (lax.rsqrt(degree) * row).astype(BF16)


def product_kernel(with_rows, place_ref, rows_ref, cols_ref, live_ref, tiles_ref, near_ref, far_ref, out_ref, acc_ref, *held):
    live = live_ref[0]
    if with_rows:
        held_ref, sems = held
        copies = tile_copies(SLOTS // GROUP, tiles_ref, held_ref, sems)
        for copy in copies:
            copy.start()
    else:
        held_ref, copies = tiles_ref, []

    def product(slot):
        col = cols_ref[slot]
        core, level = lax.rem(col, 2), lax.div(col, 2)
        if with_rows:
            at, same = level, lax.rem(core + lax.div(level, QUADS), 2) == place_ref[2]
        else:
            at = QUADS * lax.rem(level + QUADS - place_ref[1], QUADS) + lax.div(level, QUADS)
            same = core == place_ref[0]
        block = jnp.where(same, near_ref[at], far_ref[at])
        if with_rows:
            block = jnp.concatenate([block, jnp.ones((SIDE, WIDTH), BF16)], axis=1)
        block = jnp.where(slot < live, block, jnp.zeros_like(block))
        return jnp.dot(held_ref[slot], block, preferred_element_type=F32)

    for turn in range(SLOTS // GROUP):
        if copies:
            copies[turn].wait()
        slots = range(turn * GROUP, (turn + 1) * GROUP)
        for slot, value in zip(slots, [product(slot) for slot in slots]):
            if turn == 0:
                acc_ref[rows_ref[slot]] = value
            else:
                acc_ref[rows_ref[slot]] += value
    if with_rows:
        eye = eye_mask()
        zero = jnp.zeros((EXTRA - 6, WIDTH), BF16)
        for block in range(PEERS):
            out_ref[block, :SIDE] = acc_ref[block, :, :WIDTH].astype(BF16)
            pieces = []
            for half in range(2):
                spread = acc_ref[block, half * WIDTH : (half + 1) * WIDTH, WIDTH:]
                pieces.append(jnp.sum(jnp.where(eye, spread, 0.0), axis=0, keepdims=True))
            three = split3(jnp.concatenate(pieces, axis=0))
            out_ref[block, SIDE:] = jnp.concatenate(list(three) + [zero], axis=0)
    else:
        for block in range(PEERS):
            out_ref[block] = acc_ref[block].astype(BF16)


def total_of(ref, rows):
    total = ref[0, rows].astype(F32)
    for peer in range(1, PEERS):
        total += ref[peer, rows].astype(F32)
    return total


def gram_of(fresh):
    return lax.dot_general(
        fresh, fresh, (((0,), (0,)), ((), ())), precision=HIGHEST, preferred_element_type=F32
    )


def middle_kernel(arrived_ref, col_scale_ref, out_ref, row_scale_ref, gram_ref):
    extra = total_of(arrived_ref, slice(SIDE, SIDE + EXTRA))
    degree = extra[0:2] + extra[2:4] + extra[4:6]
    row_scale = lax.rsqrt(degree)
    row_scale_ref[...] = row_scale
    halves = []
    for half in range(2):
        rows = slice(half * WIDTH, (half + 1) * WIDTH)
        fresh = to_column(row_scale[half : half + 1]) * total_of(arrived_ref, rows)
        halves.append(fresh)
        out_ref[rows] = (to_column(col_scale_ref[half : half + 1]) * fresh).astype(BF16)
    gram_ref[...] = gram_of(jnp.concatenate(halves, axis=0))


def last_kernel(arrived_ref, row_scale_ref, first_gram_ref, fresh_ref, out_ref):
    halves = []
    for half in range(2):
        rows = slice(half * WIDTH, (half + 1) * WIDTH)
        fresh = to_column(row_scale_ref[half : half + 1]) * total_of(arrived_ref, rows)
        fresh_ref[rows] = fresh
        halves.append(fresh)
    gram = gram_of(jnp.concatenate(halves, axis=0))
    for peer in range(2 * PEERS):
        rows = slice(GRAM_ROWS * peer, GRAM_ROWS * (peer + 1))
        out_ref[peer, :GRAM_ROWS] = first_gram_ref[rows]
        out_ref[peer, GRAM_ROWS:] = gram[rows]


def lower_inverse(matrix):
    groups = WIDTH // 8
    parts = [matrix[8 * g : 8 * g + 8] for g in range(groups)]
    lane = lax.broadcasted_iota(jnp.int32, (8, WIDTH), 1)
    row = lax.broadcasted_iota(jnp.int32, (8, WIDTH), 0)
    out = []
    for g in range(groups):
        at = 8 * g
        panel = parts[g]
        inside = (lane >= at) & (lane < at + 8)
        cols = [jnp.broadcast_to(panel[:, at + j : at + j + 1], (8, WIDTH)) for j in range(8)]
        left = {}
        rows = []
        for i in range(8):
            for j in range(i + 1):
                left[i, j] = jnp.broadcast_to(cols[j][i : i + 1], (8, WIDTH))
            unit = jnp.where(lane == at + i, 1.0, 0.0)
            rows.append(jnp.where(inside, unit, jnp.broadcast_to(panel[i : i + 1], (8, WIDTH))))
        inverse, lower = [], {}
        for p in range(0, 8, 2):
            a, b, c = left[p, p], left[p + 1, p], left[p + 1, p + 1]
            scale = 1.0 / (a * c - b * b)
            corner, cross, pivot = c * scale, b * scale, a * scale
            inverse += [1.0 / a, pivot]
            lower[p + 1, p] = b * inverse[p]
            left[p + 1, p + 1] = c - b * lower[p + 1, p]
            for i in range(p + 2, 8):
                first = left[i, p] * corner - left[i, p + 1] * cross
                second = left[i, p + 1] * pivot - left[i, p] * cross
                lower[i, p], lower[i, p + 1] = left[i, p] * inverse[p], second
                for j in range(p + 2, i + 1):
                    left[i, j] = left[i, j] - (first * left[j, p] + second * left[j, p + 1])
                rows[i] = rows[i] - (first * rows[p] + second * rows[p + 1])
            rows[p + 1] = rows[p + 1] - lower[p + 1, p] * rows[p]
        total = jnp.zeros((8, WIDTH), F32)
        for i in range(8):
            total = jnp.where(row == i, rows[i] * lax.rsqrt(left[i, i]), total)
        out.append(jnp.where(lane <= row + at, total, 0.0))
        solved = {}
        for i in reversed(range(8)):
            solved[i] = rows[i] * inverse[i]
            for j in range(7, i, -1):
                solved[i] = solved[i] - lower[j, i] * solved[j]
        for h in range(g + 1, groups):
            even, odd = jnp.where(inside, 0.0, parts[h]), jnp.zeros((8, WIDTH), F32)
            for j in range(8):
                term = jnp.broadcast_to(parts[h][:, at + j : at + j + 1], (8, WIDTH)) * solved[j]
                if j % 2 == 0:
                    even = even - term
                else:
                    odd = odd + term
            parts[h] = even - odd
    return jnp.concatenate(out, axis=0)


def dot(a, b, dims):
    return lax.dot_general(a, b, (dims, ((), ())), precision=HIGHEST, preferred_element_type=F32)


def finish_kernel(grams_ref, fresh_ref, out_ref):
    first_gram = grams_ref[:, :GRAM_ROWS].reshape(WIDTH, WIDTH)
    gram = grams_ref[:, GRAM_ROWS:].reshape(WIDTH, WIDTH)
    first = lower_inverse(first_gram)
    gram = dot(dot(first, gram, ((1,), (0,))), first, ((1,), (1,)))
    second = lower_inverse(gram)
    fresh = dot(fresh_ref[...], first, ((1,), (1,)))
    out_ref[...] = dot(fresh, second, ((1,), (1,)))


def shape(dims, dtype):
    return jax.ShapeDtypeStruct(dims, dtype)


def shards(tile_values, tile_rows, tile_cols, live_count, initial):
    core = lax.axis_index("core")
    group = lax.rem(core + lax.axis_index("quad"), 2)
    place = jnp.stack([core, lax.axis_index("spot"), group]).astype(jnp.int32)
    groups = [[2 * z + (at + z // QUADS) % 2 for z in range(ZS)] for at in range(2)]
    levels = ("quad", "spot")
    plane = ("core", "x", "y")
    swap = [(0, 1), (1, 0)]

    with jax.named_scope("col_degree"):
        part = pl.pallas_call(
            degree_kernel,
            out_shape=shape((ZS, 8, WIDTH), F32),
            in_specs=[smem, smem, hbm, vmem],
            out_specs=vmem,
            scratch_shapes=[
                pltpu.VMEM(tile_values.shape, BF16),
                pltpu.VMEM((2 * ZS, 8, SIDE), F32),
                pltpu.SemaphoreType.DMA((DEGREE_PARTS,)),
            ],
            compiler_params=degree_params,
        )(tile_cols, live_count, tile_values, initial)
        degrees = lax.all_to_all(part, levels, 0, 0, tiled=True)
        degrees = lax.all_gather(degrees, "core", axis=0)
    with jax.named_scope("scale"):
        sent, last, col_scale = pl.pallas_call(
            scale_kernel,
            out_shape=(
                shape((SIDE, WIDTH), BF16),
                shape((ZS, WIDTH), BF16),
                shape((2, WIDTH), F32),
            ),
            in_specs=[smem] + [vmem] * 2,
            out_specs=(vmem,) * 3,
            compiler_params=params,
        )(place, degrees, initial)

    def from_level(first, second):
        steps = (first, second)
        return [
            (((z + steps[core]) % ZS) * 2 + core, z * 2 + core) for z in range(ZS) for core in range(2)
        ]

    def gather(sent):
        chips = levels + ("core",)
        mine = lax.all_gather(sent, "quad", axis=0)
        two = lax.ppermute(mine, chips, from_level(-2, 2))
        one = lax.ppermute(mine, chips, from_level(1, 1))
        three = lax.ppermute(mine, chips, from_level(-1, -1))
        near = jnp.concatenate([mine, one, two, three], axis=0)
        return near, lax.ppermute(near, "core", swap)

    def product(with_rows, parts):
        extra, width = (EXTRA, 2 * WIDTH) if with_rows else (0, WIDTH)
        scratch = [pltpu.VMEM((PEERS, SIDE, width), F32)]
        if with_rows:
            scratch += [pltpu.VMEM(tile_values.shape, BF16), pltpu.SemaphoreType.DMA((SLOTS // GROUP,))]
        return pl.pallas_call(
            functools.partial(product_kernel, with_rows),
            out_shape=shape((PEERS, SIDE + extra, WIDTH), BF16),
            in_specs=[smem] * 4 + [hbm if with_rows else vmem, vmem, vmem],
            out_specs=vmem,
            scratch_shapes=scratch,
            compiler_params=product_params if with_rows else params,
        )(place, tile_rows, tile_cols, live_count, tile_values, *parts)

    with jax.named_scope("gather_one"):
        near = lax.all_gather(sent[: SIDE - 1], levels + ("core",), axis=0, axis_index_groups=groups)
        near = jnp.concatenate([near, last[:, None]], axis=1)
        parts = near, lax.ppermute(near, "core", swap)
    with jax.named_scope("product_one"):
        partial_value = product(True, parts)
    with jax.named_scope("reduce_one"):
        arrived = lax.all_to_all(partial_value, ("x", "y"), 0, 0, tiled=True)
    with jax.named_scope("middle"):
        sent, row_scale, first_gram = pl.pallas_call(
            middle_kernel,
            out_shape=(shape((SIDE, WIDTH), BF16), shape((2, WIDTH), F32), shape((WIDTH, WIDTH), F32)),
            in_specs=[vmem] * 2,
            out_specs=(vmem,) * 3,
            compiler_params=params,
        )(arrived, col_scale)
    with jax.named_scope("gather_two"):
        parts = gather(sent)
    with jax.named_scope("product_two"):
        partial_value = product(False, parts)
    with jax.named_scope("reduce_two"):
        arrived = lax.all_to_all(partial_value, ("x", "y"), 0, 0, tiled=True)
    with jax.named_scope("last"):
        count, deep = 2 * PEERS, 2 * GRAM_ROWS
        fresh, grams = pl.pallas_call(
            last_kernel,
            out_shape=(shape((SIDE, WIDTH), F32), shape((count, deep, WIDTH), F32)),
            in_specs=[vmem] * 3,
            out_specs=(vmem,) * 2,
            compiler_params=params,
        )(arrived, row_scale, first_gram)
    with jax.named_scope("gram"):
        piece = jnp.sum(lax.all_to_all(grams, plane, 0, 0, tiled=True), axis=0)
        spread = jnp.broadcast_to(piece[None], (ZS, deep, WIDTH))
        piece = jnp.sum(lax.all_to_all(spread, levels, 0, 0, tiled=True), axis=0)
        spread = jnp.broadcast_to(piece[None], (count, deep, WIDTH))
        grams = lax.all_to_all(spread, plane, 0, 0, tiled=True)
    with jax.named_scope("finish"):
        return pl.pallas_call(
            finish_kernel,
            out_shape=shape((SIDE, WIDTH), F32),
            in_specs=[vmem] * 2,
            out_specs=vmem,
            compiler_params=params,
        )(grams, fresh)


def solution(mesh):
    devices = np.asarray(mesh.devices).reshape(QUADS, ZS // QUADS, 2, 4, 4)
    whole = ("quad", "spot", "core", "x", "y")
    fine = Mesh(devices, whole)
    in_specs = (P(whole, None, None), P(whole), P(whole), P(whole), P(whole, None))
    return jax.shard_map(
        shards, mesh=fine, in_specs=in_specs, out_specs=P(whole, None), check_vma=False
    )
```

```python
import functools

import jax
import jax.numpy as jnp
import numpy as np
from jax import lax
from jax.experimental import pallas as pl
from jax.experimental.pallas import tpu as pltpu
from jax.sharding import Mesh, PartitionSpec as P

ZS = 16
QUADS = 4
PEERS = 16
SIDE = 256
WIDTH = 128
SLOTS = 32
GROUP = 16
DEGREE_PARTS = 4
EXTRA = 16
GRAM_ROWS = 4
VMEM_BYTES = 24 * 1024 * 1024
F32 = jnp.float32
BF16 = jnp.bfloat16
HIGHEST = lax.Precision.HIGHEST

params = pltpu.CompilerParams(vmem_limit_bytes=VMEM_BYTES)
degree_params = pltpu.CompilerParams(vmem_limit_bytes=61 * 1024 * 1024)
product_params = pltpu.CompilerParams(vmem_limit_bytes=48 * 1024 * 1024)
smem = pl.BlockSpec(memory_space=pltpu.SMEM)
vmem = pl.BlockSpec(memory_space=pltpu.VMEM)
hbm = pl.BlockSpec(memory_space=pl.ANY)


def eye_mask():
    return lax.broadcasted_iota(jnp.int32, (WIDTH, WIDTH), 0) == lax.broadcasted_iota(
        jnp.int32, (WIDTH, WIDTH), 1
    )


def to_column(lanes):
    spread = jnp.broadcast_to(lanes, (WIDTH, WIDTH))
    return jnp.sum(jnp.where(eye_mask(), spread, 0.0), axis=1, keepdims=True)


def split3(value):
    high = value.astype(BF16)
    rest = value - high.astype(F32)
    middle = rest.astype(BF16)
    low = (rest - middle.astype(F32)).astype(BF16)
    return high, middle, low


def tile_copies(parts, tiles_ref, held_ref, sems):
    size = SLOTS // parts
    copies = []
    for part in range(parts):
        rows = pl.ds(part * size, size)
        copies.append(pltpu.make_async_copy(tiles_ref.at[rows], held_ref.at[rows], sems.at[part]))
    return copies


def degree_kernel(cols_ref, live_ref, tiles_ref, initial_ref, out_ref, held_ref, acc_ref, sems):
    copies = tile_copies(DEGREE_PARTS, tiles_ref, held_ref, sems)
    for copy in copies:
        copy.start()
    acc_ref[...] = jnp.zeros_like(acc_ref)
    size = SLOTS // DEGREE_PARTS

    def one(slot, carry):
        @pl.when(slot < live_ref[0])
        def _():
            tile = held_ref[slot].astype(F32).reshape(SIDE // 8, 8, SIDE)
            acc_ref[cols_ref[slot]] += jnp.sum(tile, axis=0)

        return carry

    for part, copy in enumerate(copies):
        copy.wait()
        lax.fori_loop(part * size, part * size + size, one, 0)
    lane = lax.broadcasted_iota(jnp.int32, (1, WIDTH), 1)
    last = jnp.zeros((1, WIDTH), F32)
    for block in range(2 * ZS):
        total = jnp.sum(acc_ref[block], axis=0, keepdims=True)
        at = 2 * (block % 2)
        out_ref[block // 2, at : at + 1, :] = total[:, :WIDTH]
        out_ref[block // 2, at + 1 : at + 2, :] = total[:, WIDTH:]
        last = jnp.where(lane == block, total[:, SIDE - 1 :], last)
    row = initial_ref[SIDE - 16 :].astype(F32)[15:]
    rest = jnp.concatenate([last, row, jnp.zeros((2, WIDTH), F32)], axis=0)
    for peer in range(ZS):
        out_ref[peer, 4:] = rest


def scale_kernel(place_ref, degrees_ref, initial_ref, out_ref, last_ref, scale_ref):
    both = degrees_ref[0, 0] + degrees_ref[1, 0]
    for level in range(1, ZS):
        both += degrees_ref[0, level] + degrees_ref[1, level]
    scale = lax.rsqrt(jnp.where(place_ref[0] == 0, both[0:2], both[2:4]))
    scale_ref[...] = scale
    for half in range(2):
        rows = slice(half * WIDTH, (half + 1) * WIDTH)
        column = to_column(scale[half : half + 1])
        out_ref[rows] = (column * initial_ref[rows].astype(F32)).astype(BF16)
    level = lax.broadcasted_iota(jnp.int32, (ZS, WIDTH), 0)
    lane = lax.broadcasted_iota(jnp.int32, (ZS, WIDTH), 1)
    core = lax.rem(lax.div(level, QUADS) + place_ref[2], 2)
    picked = jnp.where(lane == 2 * level + core, jnp.broadcast_to(both[4:5], (ZS, WIDTH)), 0.0)
    degree = jnp.sum(picked, axis=1, keepdims=True)
    row = jnp.where(core == 0, degrees_ref[0, :, 5, :], degrees_ref[1, :, 5, :])
    last_ref[...] = (lax.rsqrt(degree) * row).astype(BF16)


def product_kernel(with_rows, place_ref, rows_ref, cols_ref, live_ref, tiles_ref, near_ref, far_ref, out_ref, acc_ref, *held):
    live = live_ref[0]
    if with_rows:
        held_ref, sems = held
        copies = tile_copies(SLOTS // GROUP, tiles_ref, held_ref, sems)
        for copy in copies:
            copy.start()
    else:
        held_ref, copies = tiles_ref, []

    def product(slot):
        col = cols_ref[slot]
        core, level = lax.rem(col, 2), lax.div(col, 2)
        if with_rows:
            at, same = level, lax.rem(core + lax.div(level, QUADS), 2) == place_ref[2]
        else:
            at = QUADS * lax.rem(level + QUADS - place_ref[1], QUADS) + lax.div(level, QUADS)
            same = core == place_ref[0]
        block = jnp.where(same, near_ref[at], far_ref[at])
        if with_rows:
            block = jnp.concatenate([block, jnp.ones((SIDE, WIDTH), BF16)], axis=1)
        block = jnp.where(slot < live, block, jnp.zeros_like(block))
        return jnp.dot(held_ref[slot], block, preferred_element_type=F32)

    for turn in range(SLOTS // GROUP):
        if copies:
            copies[turn].wait()
        slots = range(turn * GROUP, (turn + 1) * GROUP)
        for slot, value in zip(slots, [product(slot) for slot in slots]):
            if turn == 0:
                acc_ref[rows_ref[slot]] = value
            else:
                acc_ref[rows_ref[slot]] += value
    if with_rows:
        eye = eye_mask()
        zero = jnp.zeros((EXTRA - 6, WIDTH), BF16)
        for block in range(PEERS):
            out_ref[block, :SIDE] = acc_ref[block, :, :WIDTH].astype(BF16)
            pieces = []
            for half in range(2):
                spread = acc_ref[block, half * WIDTH : (half + 1) * WIDTH, WIDTH:]
                pieces.append(jnp.sum(jnp.where(eye, spread, 0.0), axis=0, keepdims=True))
            three = split3(jnp.concatenate(pieces, axis=0))
            out_ref[block, SIDE:] = jnp.concatenate(list(three) + [zero], axis=0)
    else:
        for block in range(PEERS):
            out_ref[block] = acc_ref[block].astype(BF16)


def total_of(ref, rows):
    total = ref[0, rows].astype(F32)
    for peer in range(1, PEERS):
        total += ref[peer, rows].astype(F32)
    return total


def gram_of(fresh):
    return lax.dot_general(
        fresh, fresh, (((0,), (0,)), ((), ())), precision=HIGHEST, preferred_element_type=F32
    )


def middle_kernel(arrived_ref, col_scale_ref, out_ref, row_scale_ref, gram_ref):
    extra = total_of(arrived_ref, slice(SIDE, SIDE + EXTRA))
    degree = extra[0:2] + extra[2:4] + extra[4:6]
    row_scale = lax.rsqrt(degree)
    row_scale_ref[...] = row_scale
    halves = []
    for half in range(2):
        rows = slice(half * WIDTH, (half + 1) * WIDTH)
        fresh = to_column(row_scale[half : half + 1]) * total_of(arrived_ref, rows)
        halves.append(fresh)
        out_ref[rows] = (to_column(col_scale_ref[half : half + 1]) * fresh).astype(BF16)
    gram_ref[...] = gram_of(jnp.concatenate(halves, axis=0))


def last_kernel(arrived_ref, row_scale_ref, first_gram_ref, fresh_ref, out_ref):
    halves = []
    for half in range(2):
        rows = slice(half * WIDTH, (half + 1) * WIDTH)
        fresh = to_column(row_scale_ref[half : half + 1]) * total_of(arrived_ref, rows)
        fresh_ref[rows] = fresh
        halves.append(fresh)
    gram = gram_of(jnp.concatenate(halves, axis=0))
    for peer in range(2 * PEERS):
        rows = slice(GRAM_ROWS * peer, GRAM_ROWS * (peer + 1))
        out_ref[peer, :GRAM_ROWS] = first_gram_ref[rows]
        out_ref[peer, GRAM_ROWS:] = gram[rows]


def lower_inverse(matrix):
    groups = WIDTH // 8
    parts = [matrix[8 * g : 8 * g + 8] for g in range(groups)]
    lane = lax.broadcasted_iota(jnp.int32, (8, WIDTH), 1)
    row = lax.broadcasted_iota(jnp.int32, (8, WIDTH), 0)
    out = []
    for g in range(groups):
        at = 8 * g
        panel = parts[g]
        inside = (lane >= at) & (lane < at + 8)
        cols = [jnp.broadcast_to(panel[:, at + j : at + j + 1], (8, WIDTH)) for j in range(8)]
        left = {}
        rows = []
        for i in range(8):
            for j in range(i + 1):
                left[i, j] = jnp.broadcast_to(cols[j][i : i + 1], (8, WIDTH))
            unit = jnp.where(lane == at + i, 1.0, 0.0)
            rows.append(jnp.where(inside, unit, jnp.broadcast_to(panel[i : i + 1], (8, WIDTH))))
        inverse, lower = [], {}
        for p in range(0, 8, 2):
            a, b, c = left[p, p], left[p + 1, p], left[p + 1, p + 1]
            scale = 1.0 / (a * c - b * b)
            corner, cross, pivot = c * scale, b * scale, a * scale
            inverse += [1.0 / a, pivot]
            lower[p + 1, p] = b * inverse[p]
            left[p + 1, p + 1] = c - b * lower[p + 1, p]
            for i in range(p + 2, 8):
                first = left[i, p] * corner - left[i, p + 1] * cross
                second = left[i, p + 1] * pivot - left[i, p] * cross
                lower[i, p], lower[i, p + 1] = left[i, p] * inverse[p], second
                for j in range(p + 2, i + 1):
                    left[i, j] = left[i, j] - (first * left[j, p] + second * left[j, p + 1])
                rows[i] = rows[i] - (first * rows[p] + second * rows[p + 1])
            rows[p + 1] = rows[p + 1] - lower[p + 1, p] * rows[p]
        total = jnp.zeros((8, WIDTH), F32)
        for i in range(8):
            total = jnp.where(row == i, rows[i] * lax.rsqrt(left[i, i]), total)
        out.append(jnp.where(lane <= row + at, total, 0.0))
        solved = {}
        for i in reversed(range(8)):
            solved[i] = rows[i] * inverse[i]
            for j in range(7, i, -1):
                solved[i] = solved[i] - lower[j, i] * solved[j]
        for h in range(g + 1, groups):
            even, odd = jnp.where(inside, 0.0, parts[h]), jnp.zeros((8, WIDTH), F32)
            for j in range(8):
                term = jnp.broadcast_to(parts[h][:, at + j : at + j + 1], (8, WIDTH)) * solved[j]
                if j % 2 == 0:
                    even = even - term
                else:
                    odd = odd + term
            parts[h] = even - odd
    return jnp.concatenate(out, axis=0)


def dot(a, b, dims):
    return lax.dot_general(a, b, (dims, ((), ())), precision=HIGHEST, preferred_element_type=F32)


def finish_kernel(grams_ref, fresh_ref, out_ref):
    first_gram = grams_ref[:, :GRAM_ROWS].reshape(WIDTH, WIDTH)
    gram = grams_ref[:, GRAM_ROWS:].reshape(WIDTH, WIDTH)
    first = lower_inverse(first_gram)
    gram = dot(dot(first, gram, ((1,), (0,))), first, ((1,), (1,)))
    second = lower_inverse(gram)
    fresh = dot(fresh_ref[...], first, ((1,), (1,)))
    out_ref[...] = dot(fresh, second, ((1,), (1,)))


def shape(dims, dtype):
    return jax.ShapeDtypeStruct(dims, dtype)


def shards(tile_values, tile_rows, tile_cols, live_count, initial):
    core = lax.axis_index("core")
    group = lax.rem(core + lax.axis_index("quad"), 2)
    place = jnp.stack([core, lax.axis_index("spot"), group]).astype(jnp.int32)
    groups = [[2 * z + (at + z // QUADS) % 2 for z in range(ZS)] for at in range(2)]
    levels = ("quad", "spot")
    plane = ("core", "x", "y")
    swap = [(0, 1), (1, 0)]

    with jax.named_scope("col_degree"):
        part = pl.pallas_call(
            degree_kernel,
            out_shape=shape((ZS, 8, WIDTH), F32),
            in_specs=[smem, smem, hbm, vmem],
            out_specs=vmem,
            scratch_shapes=[
                pltpu.VMEM(tile_values.shape, BF16),
                pltpu.VMEM((2 * ZS, 8, SIDE), F32),
                pltpu.SemaphoreType.DMA((DEGREE_PARTS,)),
            ],
            compiler_params=degree_params,
        )(tile_cols, live_count, tile_values, initial)
        degrees = lax.all_to_all(part, levels, 0, 0, tiled=True)
        degrees = lax.all_gather(degrees, "core", axis=0)
    with jax.named_scope("scale"):
        sent, last, col_scale = pl.pallas_call(
            scale_kernel,
            out_shape=(
                shape((SIDE, WIDTH), BF16),
                shape((ZS, WIDTH), BF16),
                shape((2, WIDTH), F32),
            ),
            in_specs=[smem] + [vmem] * 2,
            out_specs=(vmem,) * 3,
            compiler_params=params,
        )(place, degrees, initial)

    def from_level(first, second):
        steps = (first, second)
        return [
            (((z + steps[core]) % ZS) * 2 + core, z * 2 + core) for z in range(ZS) for core in range(2)
        ]

    def gather(sent):
        chips = levels + ("core",)
        mine = lax.all_gather(sent, "quad", axis=0)
        one = lax.ppermute(mine, chips, from_level(1, 1))
        three = lax.ppermute(mine, chips, from_level(-1, -1))
        two = lax.ppermute(mine, chips, from_level(-2, 2))
        near = jnp.concatenate([mine, one, two, three], axis=0)
        return near, lax.ppermute(near, "core", swap)

    def product(with_rows, parts):
        extra, width = (EXTRA, 2 * WIDTH) if with_rows else (0, WIDTH)
        scratch = [pltpu.VMEM((PEERS, SIDE, width), F32)]
        if with_rows:
            scratch += [pltpu.VMEM(tile_values.shape, BF16), pltpu.SemaphoreType.DMA((SLOTS // GROUP,))]
        return pl.pallas_call(
            functools.partial(product_kernel, with_rows),
            out_shape=shape((PEERS, SIDE + extra, WIDTH), BF16),
            in_specs=[smem] * 4 + [hbm if with_rows else vmem, vmem, vmem],
            out_specs=vmem,
            scratch_shapes=scratch,
            compiler_params=product_params if with_rows else params,
        )(place, tile_rows, tile_cols, live_count, tile_values, *parts)

    with jax.named_scope("gather_one"):
        near = lax.all_gather(sent[: SIDE - 1], levels + ("core",), axis=0, axis_index_groups=groups)
        near = jnp.concatenate([near, last[:, None]], axis=1)
        parts = near, lax.ppermute(near, "core", swap)
    with jax.named_scope("product_one"):
        partial_value = product(True, parts)
    with jax.named_scope("reduce_one"):
        arrived = lax.all_to_all(partial_value, ("x", "y"), 0, 0, tiled=True)
    with jax.named_scope("middle"):
        sent, row_scale, first_gram = pl.pallas_call(
            middle_kernel,
            out_shape=(shape((SIDE, WIDTH), BF16), shape((2, WIDTH), F32), shape((WIDTH, WIDTH), F32)),
            in_specs=[vmem] * 2,
            out_specs=(vmem,) * 3,
            compiler_params=params,
        )(arrived, col_scale)
    with jax.named_scope("gather_two"):
        parts = gather(sent)
    with jax.named_scope("product_two"):
        partial_value = product(False, parts)
    with jax.named_scope("reduce_two"):
        arrived = lax.all_to_all(partial_value, ("x", "y"), 0, 0, tiled=True)
    with jax.named_scope("last"):
        count, deep = 2 * PEERS, 2 * GRAM_ROWS
        fresh, grams = pl.pallas_call(
            last_kernel,
            out_shape=(shape((SIDE, WIDTH), F32), shape((count, deep, WIDTH), F32)),
            in_specs=[vmem] * 3,
            out_specs=(vmem,) * 2,
            compiler_params=params,
        )(arrived, row_scale, first_gram)
    with jax.named_scope("gram"):
        piece = jnp.sum(lax.all_to_all(grams, plane, 0, 0, tiled=True), axis=0)
        spread = jnp.broadcast_to(piece[None], (ZS, deep, WIDTH))
        piece = jnp.sum(lax.all_to_all(spread, levels, 0, 0, tiled=True), axis=0)
        spread = jnp.broadcast_to(piece[None], (count, deep, WIDTH))
        grams = lax.all_to_all(spread, plane, 0, 0, tiled=True)
    with jax.named_scope("finish"):
        return pl.pallas_call(
            finish_kernel,
            out_shape=shape((SIDE, WIDTH), F32),
            in_specs=[vmem] * 2,
            out_specs=vmem,
            compiler_params=params,
        )(grams, fresh)


def solution(mesh):
    devices = np.asarray(mesh.devices).reshape(QUADS, ZS // QUADS, 2, 4, 4)
    whole = ("quad", "spot", "core", "x", "y")
    fine = Mesh(devices, whole)
    in_specs = (P(whole, None, None), P(whole), P(whole), P(whole), P(whole, None))
    return jax.shard_map(
        shards, mesh=fine, in_specs=in_specs, out_specs=P(whole, None), check_vma=False
    )
```
